128 devices in a mesh: gx: 8 (over y, core), gy: 16 (over z, x).
Axes of the slice: x: 4, y: 4, z: 4, core: 2. Of those that a mesh axis runs over, the one named last changes fastest.
Arguments:
- fine_list: int32 [16384], P(('gx', 'gy')), may hold values from -1 to 12287, as said below
- fine_residual: float32 [16384, 6, 192], P(('gx', 'gy')), may hold values from -6 to 6
- solid_bits: int32 [16384, 3], P(('gx', 'gy')), may hold values from 0 to 1073741823
- restrict_ops: float32 [8, 192, 192], replicated, may hold values from -0.4375 to 0.4375
- operator: bfloat16 [8, 16, 12, 27, 192, 192], P('gx', 'gy'), as said below
- pattern: int32 [8, 16, 12, 26], P('gx', 'gy'), may hold values from 0 to 25, each once within a row
Outputs:
- fine_correction: float32 [16384, 6, 192], P(('gx', 'gy'))
- coarse_solution: float32 [8, 16, 12, 6, 192], P('gx', 'gy')
The draws below stay inside these ranges and needn't reach their ends.
Inputs may be any that keep to these rules, and one draw needn't show every extreme that they name: `fine_list`: an entry 8 c + o names coarse brick c and octant o; -1 marks an empty slot. Every live entry of a device names a coarse brick owned by that device or by one of the devices next to it along gx, gy or both, the owner of brick (X, Y, Z) being the device with index X // 1 along gx and Y // 1 along gy. `operator`: block 0 of each row is the brick's own block; the other 26 blocks act on the neighbours in the order that pattern gives. The own blocks' diagonal entries are at least 0.6.
All inputs are finite; a program needn't handle non-finite values.
Results may differ from the reference program's by a relative error of at most 0.015.
Values may be sent and summed in bfloat16 or wider, within the bound.
A program may use at most 128 MiB of HBM per device.

```python
import math
import jax
import jax.numpy as jnp
import numpy as np
from jax import lax

BRICK_VALUES = 192
LOADS = 6
NBR = 27
SWEEPS = 8
CBXY = 1
CBZ = 12
FB_DEV = 128
WORDS = 3
NCX = 8
NCY = 16
FB_TOTAL = 16384


def draw_fine_list(key, part):
    subkeys = jax.random.split(jax.random.fold_in(key, 11), 5)
    grid_x = NCX // CBXY
    grid_y = NCY // CBXY
    devices = grid_x * grid_y
    source = jnp.arange(FB_TOTAL, dtype=jnp.int32) // FB_DEV
    src_x = source // grid_y
    src_y = source % grid_y
    live_rate = jax.random.randint(subkeys[0], (devices,), 2, 9)
    coin_flip = jax.random.randint(subkeys[1], (FB_TOTAL,), 0, 8)
    occupied = coin_flip < live_rate[source]
    pick = jax.random.randint(subkeys[2], (FB_TOTAL,), 0, 10)
    neighbour = jnp.maximum(pick - 2, 0)
    near = neighbour + (neighbour >= 4).astype(jnp.int32)
    step_x = jnp.where(pick < 2, 0, near // 3 - 1)
    step_y = jnp.where(pick < 2, 0, near % 3 - 1)
    owner_x = jnp.clip(src_x + step_x, 0, grid_x - 1)
    owner_y = jnp.clip(src_y + step_y, 0, grid_y - 1)
    local_brick = jax.random.randint(subkeys[3], (FB_TOTAL,), 0, CBXY * CBXY * CBZ)
    octant = jax.random.randint(subkeys[4], (FB_TOTAL,), 0, 8)
    pos_x = owner_x * CBXY + local_brick // (CBXY * CBZ)
    pos_y = owner_y * CBXY + local_brick // CBZ % CBXY
    pos_z = local_brick % CBZ
    coarse = (pos_x * NCY + pos_y) * CBZ + pos_z
    return jnp.where(occupied, coarse * 8 + octant, -1).astype(jnp.int32)


def draw_operator(key, part):
    subkeys = jax.random.split(jax.random.fold_in(key, 23), 2)
    shape = (NCX, NCY, CBZ, NBR, BRICK_VALUES, BRICK_VALUES)
    spread = 1.0 / math.sqrt(NBR * BRICK_VALUES)
    values = jax.random.normal(subkeys[0], shape, jnp.float32) * (0.7 * spread)
    diagonal = jax.random.uniform(subkeys[1], (NCX, NCY, CBZ, 1, BRICK_VALUES, 1), jnp.float32, 0.6, 1.0)
    row_iota = lax.broadcasted_iota(jnp.int32, (1, 1, 1, 1, BRICK_VALUES, BRICK_VALUES), 4)
    col_iota = lax.broadcasted_iota(jnp.int32, (1, 1, 1, 1, BRICK_VALUES, BRICK_VALUES), 5)
    block_iota = lax.broadcasted_iota(jnp.int32, (1, 1, 1, NBR, 1, 1), 3)
    on_diagonal = jnp.logical_and(row_iota == col_iota, block_iota == 0)
    return jnp.where(on_diagonal, diagonal, values).astype(jnp.bfloat16)


def plant(result, own_key, low, largest):
    spot = [jax.random.randint(jax.random.fold_in(own_key, axis), (), 0, length) for axis, length in enumerate(result.shape)]
    widest = result.shape.index(max(result.shape))
    beside = spot[:widest] + [(spot[widest] + 1) % result.shape[widest]] + spot[widest + 1:]
    return result.at[tuple(spot)].set(low).at[tuple(beside)].set(largest)


def shard_levels(own_key, dims, cuts, smallest, top_value):
    level = 1.0
    for dim, shards_of in cuts:
        steps = jax.random.uniform(jax.random.fold_in(jax.random.fold_in(own_key, 6), dim), (shards_of,), jnp.float32, smallest / len(cuts), top_value / len(cuts))
        level = level * jnp.repeat(jnp.exp(steps), dims[dim] // shards_of).reshape((-1,) + (1,) * (len(dims) - 1 - dim))
    return level


def scatter_about(rng, dims, scale, most, shards=(), held_as=jnp.bfloat16):
    factor_of = shard_levels(rng, dims, shards, -0.22, 0.18) if shards else 1.0
    result = jax.random.normal(rng, dims, jnp.float32) * scale * factor_of
    return jnp.minimum(jnp.maximum(result, -most), most).astype(held_as)


def setup_inputs(seed: int = 0) -> dict:
    arg_keys = jax.random.split(jax.random.key(seed), 7)
    fine_list = draw_fine_list(jax.random.fold_in(arg_keys[6], 71), 0)
    fine_residual = scatter_about(arg_keys[1], (FB_TOTAL, LOADS, BRICK_VALUES), 1.0, 6.0, ((0, 128),), jnp.float32)
    solid_bits = plant(jax.random.randint(arg_keys[2], (FB_TOTAL, WORDS), 0, 1073741824), jax.random.fold_in(arg_keys[2], 1), 0, 1073741823).astype(jnp.int32)
    restrict_ops = scatter_about(arg_keys[3], (8, BRICK_VALUES, BRICK_VALUES), BRICK_VALUES ** -0.5, 0.4375, (), jnp.float32)
    operator = draw_operator(jax.random.fold_in(arg_keys[6], 71), 0)
    pattern = jax.vmap(lambda own: jax.random.permutation(own, 26))(jax.random.split(arg_keys[5], NCX * NCY * CBZ)).reshape((NCX, NCY, CBZ, NBR - 1)).astype(jnp.int32)
    return {"fine_list": fine_list, "fine_residual": fine_residual, "solid_bits": solid_bits, "restrict_ops": restrict_ops, "operator": operator, "pattern": pattern}


damping = 0.8


def value_mask(solid_bits, brick_values):
    node_count = brick_values // 3
    node_ids = np.arange(node_count)
    word_values = solid_bits[:, node_ids // 30]
    shifts = jnp.asarray(node_ids % 30, dtype=jnp.int32)
    node_flags = jnp.bitwise_and(jnp.right_shift(word_values, shifts[None, :]), 1).astype(jnp.float32)
    return jnp.concatenate([node_flags, node_flags, node_flags], axis=1)


def neighbour_index(pattern, span_x, span_y, span_z):
    offset = pattern + (pattern >= 13).astype(jnp.int32)
    own_zero = jnp.zeros((span_x, span_y, span_z, 1), jnp.int32)
    step_x = jnp.concatenate([own_zero, offset // 9 - 1], axis=3)
    step_y = jnp.concatenate([own_zero, (offset // 3) % 3 - 1], axis=3)
    step_z = jnp.concatenate([own_zero, offset % 3 - 1], axis=3)
    base_x = lax.broadcasted_iota(jnp.int32, (span_x, span_y, span_z, 1), 0)
    base_y = lax.broadcasted_iota(jnp.int32, (span_x, span_y, span_z, 1), 1)
    base_z = lax.broadcasted_iota(jnp.int32, (span_x, span_y, span_z, 1), 2)
    return ((base_x + 1 + step_x) * (span_y + 2) + (base_y + 1 + step_y)) * (span_z + 2) + (base_z + 1 + step_z)


def octant_apply(rows_in, octant, restrict_ops, transpose):
    row_count = rows_in.shape[0]
    block_rows = 256 if row_count % 256 == 0 else row_count
    einsum_form = 'kji,klj->kli' if transpose else 'kij,klj->kli'

    def one_block(inputs):
        values, chosen_octant = inputs
        chosen = restrict_ops[chosen_octant]
        return jnp.einsum(einsum_form, chosen, values, precision=lax.Precision.HIGHEST)

    shaped = (rows_in.reshape(row_count // block_rows, block_rows, rows_in.shape[1], rows_in.shape[2]),
              octant.reshape(row_count // block_rows, block_rows))
    return lax.map(one_block, shaped).reshape(rows_in.shape)


def apply_operator(rounded, operator, pattern):
    span_x, span_y, span_z = rounded.shape[0], rounded.shape[1], rounded.shape[2]
    padded = jnp.pad(rounded, ((1, 1), (1, 1), (1, 1), (0, 0), (0, 0)))
    flat_rows = padded.reshape(-1, rounded.shape[3], rounded.shape[4])
    row_index = neighbour_index(pattern, span_x, span_y, span_z)

    def one_column(inputs):
        blocks, row_ids = inputs
        beside_all = flat_rows[row_ids].astype(jnp.float32)
        return jnp.einsum('yzkij,yzklj->yzli', blocks.astype(jnp.float32), beside_all,
                          precision=lax.Precision.HIGHEST)

    return lax.map(one_column, (operator, row_index))


def reference(fine_list, fine_residual, solid_bits, restrict_ops, operator, pattern):
    brick_values = restrict_ops.shape[1]
    load_cases = fine_residual.shape[1]
    occupied = fine_list >= 0
    coarse_index = jnp.where(occupied, fine_list // 8, 0).astype(jnp.int32)
    octant = (fine_list % 8).astype(jnp.int32)
    fine_mask = value_mask(solid_bits, brick_values) * occupied[:, None].astype(jnp.float32)
    masked = fine_residual * fine_mask[:, None, :]
    restricted = octant_apply(masked, octant, restrict_ops, False)
    bricks = NCX * NCY * CBZ
    target = jnp.where(occupied, coarse_index, bricks).astype(jnp.int32)
    coarse_rhs = jax.ops.segment_sum(restricted, target, num_segments=bricks + 1)[:bricks]
    coarse_rhs = coarse_rhs.reshape(NCX, NCY, CBZ, load_cases, brick_values)
    diag_values = jnp.diagonal(operator[:, :, :, 0], axis1=-2, axis2=-1).astype(jnp.float32)
    step_scale = damping / diag_values[:, :, :, None, :]
    coarse_solution = step_scale * coarse_rhs
    for step_index in range(SWEEPS - 1):
        rounded = coarse_solution.astype(jnp.bfloat16)
        applied = apply_operator(rounded, operator, pattern)
        coarse_solution = coarse_solution + step_scale * (coarse_rhs - applied)
    solution_rows = coarse_solution.reshape(bricks, load_cases, brick_values)
    fetched = solution_rows[coarse_index]
    fine_correction = octant_apply(fetched, octant, restrict_ops, True) * fine_mask[:, None, :]
    return fine_correction, coarse_solution
```

```python
import functools
import jax
import jax.numpy as jnp
from jax import lax
from jax.experimental import pallas as pl
from jax.experimental.pallas import tpu as pltpu
from jax.sharding import PartitionSpec as P

SWEEPS = 8
DAMPING = 0.8
OFFSETS = [(dx, dy) for dx in (-1, 0, 1) for dy in (-1, 0, 1)]
OWN = 4
SLOT = {d: (d if d < OWN else d - 1) for d in range(9) if d != OWN}
SLOT[OWN] = 8
ZERO = 9
JOINED = ((0, 1), (2, 3), (5, 6), (7, 8))
NT = (((1,), (1,)), ((), ()))
F32 = jnp.float32
BF16 = jnp.bfloat16


def dot(a, b):
    return jnp.dot(a, b, preferred_element_type=F32)


def dot_nt(a, b):
    return lax.dot_general(a, b, NT, preferred_element_type=F32)


def swapped(tile):
    return jnp.concatenate([tile[8:16], tile[0:8]], axis=0)


def kernel(
    list_hbm, bits_hbm, residual_hbm, restrict_hbm, operator_hbm, pattern_hbm,
    correction_ref, coarse_ref,
    list_v, bits_v, residual_v, restrict_v, own_v, pattern_v, inverse_v, inverse_s,
    packed, restrict_b, restrict_t, gather_v, rhs_own, rhs_send, rhs_land,
    land, turned, joined, solution_v, rhs_v, scale_v,
    small_sem, raw_sem, inverse_sem, rhs_sems, send_sems, recv_sems,
    *raw,
):
    bricks = len(raw)
    pairs = bricks // 2
    loads = residual_v.shape[0]
    values = restrict_v.shape[1]
    slots = list_v.shape[1]
    rows = bricks * 8
    count_x = lax.axis_size("gx")
    count_y = lax.axis_size("gy")
    here_x = lax.axis_index("gx")
    here_y = lax.axis_index("gy")

    small = [
        pltpu.make_async_copy(src, dst, small_sem.at[i])
        for i, (src, dst) in enumerate(
            [
                (pattern_hbm, pattern_v),
                (list_hbm, list_v),
                (bits_hbm, bits_v),
                (residual_hbm, residual_v),
                (restrict_hbm, restrict_v),
                (operator_hbm.at[:, 0], own_v),
            ]
        )
    ]
    for copy in small:
        copy.start()
    big = [
        pltpu.make_async_copy(operator_hbm.at[c, pl.ds(1, 26)], raw[c], raw_sem.at[c])
        for c in range(bricks)
    ]
    for copy in big:
        copy.start()

    targets = []
    inside = []
    for d, (dx, dy) in enumerate(OFFSETS):
        to_x = here_x + dx
        to_y = here_y + dy
        inside.append((to_x >= 0) & (to_x < count_x) & (to_y >= 0) & (to_y < count_y))
        targets.append((lax.rem(to_x + count_x, count_x), lax.rem(to_y + count_y, count_y)))
    barrier = pltpu.get_barrier_semaphore()
    for d in range(9):
        if d != OWN:
            pl.semaphore_signal(
                barrier, inc=1, device_id=targets[d], device_id_type=pl.DeviceIdType.MESH
            )

    for par in range(2):
        land[par, ZERO] = jnp.zeros(land.shape[2:], BF16)

    small[0].wait()
    pattern = pattern_v[...].reshape(bricks, 26)
    lane = lax.broadcasted_iota(jnp.int32, (bricks, 26), 1)
    wide = lax.broadcasted_iota(jnp.int32, (bricks, 128), 1)
    inverse = jnp.zeros((bricks, 128), jnp.int32)
    for t in range(26):
        at = jnp.max(jnp.where(pattern == t, lane, 0), axis=1, keepdims=True)
        inverse = jnp.where(wide == t, at, inverse)
    inverse_v[...] = jnp.zeros(inverse_v.shape, jnp.int32)
    inverse_v[0:bricks] = inverse
    inverse_copy = pltpu.make_async_copy(inverse_v, inverse_s, inverse_sem)
    inverse_copy.start()

    small[1].wait()
    small[2].wait()
    entry = list_v[...]
    live = entry >= 0
    brick = entry >> 3
    octant = jnp.where(live, entry & 7, -1)
    line = (brick * 43691) >> 19
    pos_z = brick - line * bricks
    step_x = (line >> 4) - here_x
    step_y = (line & 15) - here_y
    dest = ((step_x + 1) * 3 + step_y + 1) * bricks + pos_z
    dest = jnp.where(live, dest, -8)

    node = lax.broadcasted_iota(jnp.int32, (values // 3, slots), 0)
    word = jnp.where(
        node < 30, bits_v[0:1, :], jnp.where(node < 60, bits_v[1:2, :], bits_v[2:3, :])
    )
    shift = node - jnp.where(node >= 30, 30, 0) - jnp.where(node >= 60, 30, 0)
    flags = (lax.shift_right_logical(word, shift) & 1).astype(F32)
    flags = jnp.where(live, flags, 0.0)
    mask = jnp.concatenate([flags, flags, flags], axis=0)

    small[3].wait()
    masked = jnp.concatenate(
        [(residual_v[l] * mask).astype(BF16) for l in range(loads)], axis=1
    )
    small[4].wait()
    octants = jnp.concatenate([octant] * loads, axis=1)
    restricted = jnp.zeros((values, loads * slots), F32)
    for o in range(8):
        matrix = restrict_v[o].astype(BF16)
        restrict_b[o] = matrix
        chosen = masked * jnp.where(octants == o, 1.0, 0.0).astype(BF16)
        restricted += dot(matrix, chosen)
    key = jnp.concatenate([dest * 8 + l for l in range(loads)], axis=1)
    row_id = lax.broadcasted_iota(jnp.int32, (9 * rows, loads * slots), 0)
    summing = jnp.where(row_id == key, 1.0, 0.0).astype(BF16)
    outgoing = dot_nt(summing, restricted.astype(BF16))
    for d in range(9):
        part = outgoing[d * rows : (d + 1) * rows]
        tail = jnp.concatenate([part[:, 128:values], jnp.zeros((rows, 256 - values), F32)], axis=1)
        if d == OWN:
            rhs_own[:, 0:128] = part[:, 0:128]
            rhs_own[:, 128:256] = tail
        else:
            rhs_send[SLOT[d], :, 0:128] = part[:, 0:128].astype(BF16)
            rhs_send[SLOT[d], :, 128:256] = tail.astype(BF16)
    pl.semaphore_wait(barrier, 8)
    for d in range(9):
        if d != OWN:
            pltpu.make_async_remote_copy(
                src_ref=rhs_send.at[SLOT[d]],
                dst_ref=rhs_land.at[SLOT[8 - d]],
                send_sem=rhs_sems.at[0],
                recv_sem=rhs_sems.at[1],
                device_id=targets[d],
                device_id_type=pl.DeviceIdType.MESH,
            ).start()

    inverse_copy.wait()
    small[5].wait()

    def block_of(c, d, dz):
        t = d * 3 + dz + 1
        if t == 13:
            return own_v.at[c]
        return raw[c].at[inverse_s[c, t - (1 if t > 13 else 0)]]

    def repack(c):
        big[c].wait()
        partner = 1 if c % 2 == 0 else -1
        edge = c == 0 or c == bricks - 1
        at = 0
        for d in range(9):
            here = block_of(c, d, 0)
            beside = block_of(c, d, partner)
            packed[c, :, at * 128 : (at + 1) * 128] = here[:, 0:128]
            packed[c, :, (at + 1) * 128 : (at + 2) * 128] = beside[:, 0:128]
            packed[c, :, (at + 2) * 128 : (at + 3) * 128] = jnp.concatenate(
                [here[:, 128:values], beside[:, 128:values]], axis=1
            )
            at += 3
            if not edge:
                packed[c, :, at * 128 : (at + 1) * 128] = block_of(c, d, -partner)[:, 0:128]
                at += 1
        if not edge:
            for d, e in JOINED:
                packed[c, :, at * 128 : (at + 1) * 128] = jnp.concatenate(
                    [
                        block_of(c, d, -partner)[:, 128:values],
                        block_of(c, e, -partner)[:, 128:values],
                    ],
                    axis=1,
                )
                at += 1
            last = block_of(c, OWN, -partner)[:, 128:values]
            packed[c, :, at * 128 : (at + 1) * 128] = jnp.concatenate(
                [last, jnp.zeros_like(last)], axis=1
            )

    for c in range(4):
        repack(c)

    square = lax.broadcasted_iota(jnp.int32, (slots, slots), 0) == lax.broadcasted_iota(
        jnp.int32, (slots, slots), 1
    )

    def upright(row):
        return jnp.sum(
            jnp.where(square, row.astype(F32), 0.0), axis=1, keepdims=True
        ).astype(jnp.int32)

    dest_up = upright(dest)
    column_id = lax.broadcasted_iota(jnp.int32, (slots, 9 * rows), 1)
    for l in range(loads):
        gather_v[l * slots : (l + 1) * slots, :] = jnp.where(
            column_id == dest_up * 8 + l, 1.0, 0.0
        ).astype(BF16)
    diagonal = lax.broadcasted_iota(jnp.int32, (values, values), 0) == lax.broadcasted_iota(
        jnp.int32, (values, values), 1
    )
    unit = jnp.where(diagonal, 1.0, 0.0).astype(BF16)
    for o in range(8):
        restrict_t[o] = dot_nt(unit, restrict_b[o]).astype(BF16)

    for p in range(pairs):
        halves = []
        for c in (2 * p, 2 * p + 1):
            found = jnp.sum(
                jnp.where(diagonal, own_v[c].astype(F32), 0.0), axis=0, keepdims=True
            )
            halves.append(jnp.broadcast_to(DAMPING / found, (8, values)))
        scale = jnp.concatenate(halves, axis=0)
        scale_v[p, :, 0:128] = scale[:, 0:128]
        scale_v[p, :, 128:256] = jnp.concatenate(
            [scale[:, 128:values], jnp.zeros((16, 256 - values), F32)], axis=1
        )

    low = lax.broadcasted_iota(jnp.int32, (16, 128), 1) < 64

    def publish(par, p, value):
        tail = value[:, 128:256]
        land[par, SLOT[OWN], p, 0] = value[:, 0:128].astype(BF16)
        land[par, SLOT[OWN], p, 1] = jnp.where(
            low, tail, pltpu.roll(swapped(tail), 64, 1)
        ).astype(BF16)

    def send(par, q):
        for d in range(9):
            if d != OWN:
                source = jnp.where(inside[d], SLOT[OWN], ZERO)
                pltpu.make_async_remote_copy(
                    src_ref=land.at[par, source, pl.ds(2 * q, 2)],
                    dst_ref=land.at[par, SLOT[8 - d], pl.ds(2 * q, 2)],
                    send_sem=send_sems.at[par, q],
                    recv_sem=recv_sems.at[par, q],
                    device_id=targets[d],
                    device_id_type=pl.DeviceIdType.MESH,
                ).start()

    def wait_chunk(par, q, sems):
        part = land.at[par, pl.ds(0, 8), pl.ds(2 * q, 2)]
        pltpu.make_async_copy(part, part, sems.at[par, q]).wait()

    pltpu.make_async_copy(rhs_land, rhs_land, rhs_sems.at[1]).wait()
    for p in range(pairs):
        rhs = rhs_own[16 * p : 16 * p + 16, :]
        for s in range(8):
            rhs += rhs_land[s, 16 * p : 16 * p + 16, :].astype(F32)
        rhs_v[p] = rhs
        first = scale_v[p] * rhs
        solution_v[p] = first
        publish(0, p, first)
    for q in range(3):
        send(0, q)
    pltpu.make_async_copy(rhs_send, rhs_send, rhs_sems.at[0]).wait()

    for c in range(4, bricks):
        repack(c)

    def expand(par, q):
        for p in (2 * q, 2 * q + 1):
            for d in range(9):
                turned[d, p] = swapped(land[par, SLOT[d], p, 0].astype(F32)).astype(BF16)
            for i, (d, e) in enumerate(JOINED + ((OWN, OWN),)):
                left = land[par, SLOT[d], p, 1].astype(F32)
                right = land[par, SLOT[e], p, 1].astype(F32)
                joined[i, p] = jnp.where(low, pltpu.roll(left, 64, 1), right).astype(BF16)

    def apply(par, c):
        p = c // 2
        other = p - 1 if c % 2 == 0 else p + 1
        edge = c == 0 or c == bricks - 1
        tiles = []
        for d in range(9):
            tiles += [land[par, SLOT[d], p, 0], turned[d, p], land[par, SLOT[d], p, 1]]
            if not edge:
                tiles.append(turned[d, other])
        if not edge:
            tiles += [joined[i, other] for i in range(5)]
        depth = 128 * len(tiles)
        return dot_nt(jnp.concatenate(tiles, axis=1), packed[c, :, 0:depth])

    def step(e, carry):
        now = lax.rem(e, 2)
        later = 1 - now

        def finish(p, even, odd):
            applied = jnp.concatenate([even[0:8], odd[8:16]], axis=0)
            applied = jnp.concatenate([applied, jnp.zeros((16, 256 - values), F32)], axis=1)
            value = solution_v[p] + scale_v[p] * (rhs_v[p] - applied)
            solution_v[p] = value
            publish(later, p, value)

        for q in range(3):
            for c in range(4 * q, 4 * q + 4):
                if c == 0:
                    wait_chunk(now, 0, recv_sems)
                    expand(now, 0)
                if c % 4 == 3 and q < 2:
                    wait_chunk(now, q + 1, recv_sems)
                    expand(now, q + 1)
                result = apply(now, c)
                if c % 2 == 0:
                    even = result
                else:
                    finish(c // 2, even, result)
            send(later, q)
            wait_chunk(now, q, send_sems)
        return carry

    lax.fori_loop(0, SWEEPS - 1, step, 0)

    end = (SWEEPS - 1) % 2
    for p in range(pairs):
        for half in range(2):
            coarse_ref[2 * p + half] = solution_v[p, 8 * half : 8 * half + loads, 0:values]
    for q in range(3):
        wait_chunk(end, q, recv_sems)
        wait_chunk(end, q, send_sems)
    around = jnp.concatenate(
        [
            jnp.concatenate([land[end, SLOT[d], p, 0], land[end, SLOT[d], p, 1]], axis=1)
            for d in range(9)
            for p in range(pairs)
        ],
        axis=0,
    )
    fetched = dot(gather_v[...], around)[:, 0:values].astype(BF16)
    octant_up = jnp.concatenate([upright(octant)] * loads, axis=0)
    total = jnp.zeros((values, loads * slots), F32)
    for o in range(8):
        chosen = fetched * jnp.where(octant_up == o, 1.0, 0.0).astype(BF16)
        total += dot_nt(restrict_t[o], chosen)
    for l in range(loads):
        correction_ref[l] = total[:, l * slots : (l + 1) * slots] * mask


def local(fine_list, fine_residual, solid_bits, restrict_ops, operator, pattern):
    slots, loads, values = fine_residual.shape
    bricks = operator.shape[2]
    pairs = bricks // 2
    rows = bricks * 8
    any_space = pl.BlockSpec(memory_space=pl.ANY)
    vmem = pl.BlockSpec(memory_space=pltpu.VMEM)
    dma = pltpu.SemaphoreType.DMA
    correction, coarse = pl.pallas_call(
        kernel,
        out_shape=[
            jax.ShapeDtypeStruct((loads, values, slots), F32),
            jax.ShapeDtypeStruct((bricks, loads, values), F32),
        ],
        in_specs=[any_space] * 6,
        out_specs=[vmem, vmem],
        scratch_shapes=[
            pltpu.VMEM((1, slots), jnp.int32),
            pltpu.VMEM((3, slots), jnp.int32),
            pltpu.VMEM((loads, values, slots), F32),
            pltpu.VMEM((8, values, values), F32),
            pltpu.VMEM((bricks, values, values), BF16),
            pltpu.VMEM((bricks, 1, 26), jnp.int32),
            pltpu.VMEM((16, 128), jnp.int32),
            pltpu.SMEM((16, 128), jnp.int32),
            pltpu.VMEM((bricks, values, 41 * 128), BF16),
            pltpu.VMEM((8, values, values), BF16),
            pltpu.VMEM((8, values, values), BF16),
            pltpu.VMEM((loads * slots, 9 * rows), BF16),
            pltpu.VMEM((rows, 256), F32),
            pltpu.VMEM((8, rows, 256), BF16),
            pltpu.VMEM((8, rows, 256), BF16),
            pltpu.VMEM((2, 10, pairs, 2, 16, 128), BF16),
            pltpu.VMEM((9, pairs, 16, 128), BF16),
            pltpu.VMEM((5, pairs, 16, 128), BF16),
            pltpu.VMEM((pairs, 16, 256), F32),
            pltpu.VMEM((pairs, 16, 256), F32),
            pltpu.VMEM((pairs, 16, 256), F32),
            dma((6,)),
            dma((bricks,)),
            dma,
            dma((2,)),
            dma((2, 3)),
            dma((2, 3)),
        ]
        + [pltpu.VMEM((26, values, values), BF16)] * bricks,
        compiler_params=pltpu.CompilerParams(
            collective_id=0, has_side_effects=True, vmem_limit_bytes=63 * 2**20
        ),
    )(
        fine_list.reshape(1, slots),
        solid_bits.T,
        fine_residual.transpose(1, 2, 0),
        restrict_ops,
        operator.reshape(bricks, 27, values, values),
        pattern.reshape(bricks, 1, 26),
    )
    return correction.transpose(2, 0, 1), coarse.reshape(1, 1, bricks, loads, values)


def solution(mesh):
    in_specs = (
        P(("gx", "gy")),
        P(("gx", "gy"), None, None),
        P(("gx", "gy"), None),
        P(),
        P("gx", "gy", None, None, None, None),
        P("gx", "gy", None, None),
    )
    out_specs = (P(("gx", "gy"), None, None), P("gx", "gy", None, None, None))
    return jax.shard_map(local, mesh=mesh, in_specs=in_specs, out_specs=out_specs, check_vma=False)
```

```python
import functools
import jax
import jax.numpy as jnp
from jax import lax
from jax.experimental import pallas as pl
from jax.experimental.pallas import tpu as pltpu
from jax.sharding import PartitionSpec as P

SWEEPS = 8
DAMPING = 0.8
OFFSETS = [(dx, dy) for dx in (-1, 0, 1) for dy in (-1, 0, 1)]
OWN = 4
AHEAD = 4
SLOT = {d: (d if d < OWN else d - 1) for d in range(9) if d != OWN}
JOINED = ((0, 1), (2, 3), (5, 6), (7, 8))
NT = (((1,), (1,)), ((), ()))
F32 = jnp.float32
BF16 = jnp.bfloat16


def dot(a, b):
    return jnp.dot(a, b, preferred_element_type=F32)


def dot_nt(a, b):
    return lax.dot_general(a, b, NT, preferred_element_type=F32)


def swapped(tile):
    return jnp.concatenate([tile[8:16], tile[0:8]], axis=0)


def kernel(
    list_hbm, bits_hbm, residual_hbm, restrict_hbm, operator_hbm, pattern_hbm,
    correction_ref, coarse_ref,
    list_v, bits_v, residual_v, restrict_v, own_v, pattern_v, inverse_v, inverse_s,
    packed, restrict_b, restrict_t, gather_v, rhs_own, rhs_send, rhs_land,
    land, own, turned, joined, solution_v, rhs_v, scale_v,
    small_sem, raw_sem, inverse_sem, rhs_sems, send_sems, recv_sems,
    *raw,
):
    bricks = len(raw)
    pairs = bricks // 2
    loads = residual_v.shape[0]
    values = restrict_v.shape[1]
    slots = list_v.shape[1]
    rows = bricks * 8
    count_x = lax.axis_size("gx")
    count_y = lax.axis_size("gy")
    here_x = lax.axis_index("gx")
    here_y = lax.axis_index("gy")

    small = [
        pltpu.make_async_copy(src, dst, small_sem.at[i])
        for i, (src, dst) in enumerate(
            [
                (pattern_hbm, pattern_v),
                (list_hbm, list_v),
                (bits_hbm, bits_v),
                (residual_hbm, residual_v),
                (restrict_hbm, restrict_v),
                (operator_hbm.at[:, 0], own_v),
            ]
        )
    ]
    for copy in small:
        copy.start()
    big = [
        pltpu.make_async_copy(operator_hbm.at[c, pl.ds(1, 26)], raw[c], raw_sem.at[c])
        for c in range(bricks)
    ]

    land[...] = jnp.zeros(land.shape, BF16)
    rhs_land[...] = jnp.zeros(rhs_land.shape, BF16)

    inside = {}
    around_x = 3 - (here_x == 0).astype(jnp.int32) - (here_x == count_x - 1).astype(jnp.int32)
    around_y = 3 - (here_y == 0).astype(jnp.int32) - (here_y == count_y - 1).astype(jnp.int32)
    beside = around_x * around_y - 1
    for d, (dx, dy) in enumerate(OFFSETS):
        to_x = here_x + dx
        to_y = here_y + dy
        if d != OWN:
            inside[d] = (to_x >= 0) & (to_x < count_x) & (to_y >= 0) & (to_y < count_y)

    def to_each(action):
        for d, (dx, dy) in enumerate(OFFSETS):
            if d != OWN:

                @pl.when(inside[d])
                def _():
                    action(d, (here_x + dx, here_y + dy))

    def wait_each(part, sem):
        for count in (8, 5, 3):

            @pl.when(beside == count)
            def _():
                some = part.at[pl.ds(0, count)]
                pltpu.make_async_copy(some, some, sem).wait()

    barrier = pltpu.get_barrier_semaphore()
    to_each(
        lambda d, target: pl.semaphore_signal(
            barrier, inc=1, device_id=target, device_id_type=pl.DeviceIdType.MESH
        )
    )

    small[0].wait()
    pattern = pattern_v[...].reshape(bricks, 26)
    lane = lax.broadcasted_iota(jnp.int32, (bricks, 26), 1)
    wide = lax.broadcasted_iota(jnp.int32, (bricks, 128), 1)
    inverse = jnp.zeros((bricks, 128), jnp.int32)
    for t in range(26):
        at = jnp.max(jnp.where(pattern == t, lane, 0), axis=1, keepdims=True)
        inverse = jnp.where(wide == t, at, inverse)
    inverse_v[...] = jnp.zeros(inverse_v.shape, jnp.int32)
    inverse_v[0:bricks] = inverse
    inverse_copy = pltpu.make_async_copy(inverse_v, inverse_s, inverse_sem)
    inverse_copy.start()

    small[1].wait()
    small[2].wait()
    entry = list_v[...]
    live = entry >= 0
    brick = entry >> 3
    octant = jnp.where(live, entry & 7, -1)
    line = (brick * 43691) >> 19
    pos_z = brick - line * bricks
    step_x = (line >> 4) - here_x
    step_y = (line & 15) - here_y
    dest = ((step_x + 1) * 3 + step_y + 1) * bricks + pos_z
    dest = jnp.where(live, dest, -8)

    node = lax.broadcasted_iota(jnp.int32, (values // 3, slots), 0)
    word = jnp.where(
        node < 30, bits_v[0:1, :], jnp.where(node < 60, bits_v[1:2, :], bits_v[2:3, :])
    )
    shift = node - jnp.where(node >= 30, 30, 0) - jnp.where(node >= 60, 30, 0)
    flags = (lax.shift_right_logical(word, shift) & 1).astype(F32)
    flags = jnp.where(live, flags, 0.0)
    mask = jnp.concatenate([flags, flags, flags], axis=0)

    small[3].wait()
    masked = jnp.concatenate(
        [(residual_v[l] * mask).astype(BF16) for l in range(loads)], axis=1
    )
    small[4].wait()
    for c in range(AHEAD):
        big[c].start()
    octants = jnp.concatenate([octant] * loads, axis=1)
    restricted = jnp.zeros((values, loads * slots), F32)
    for o in range(8):
        matrix = restrict_v[o].astype(BF16)
        restrict_b[o] = matrix
        chosen = masked * jnp.where(octants == o, 1.0, 0.0).astype(BF16)
        restricted += dot(matrix, chosen)
    key = jnp.concatenate([dest * 8 + l for l in range(loads)], axis=1)
    row_id = lax.broadcasted_iota(jnp.int32, (9 * rows, loads * slots), 0)
    summing = jnp.where(row_id == key, 1.0, 0.0).astype(BF16)
    outgoing = dot_nt(summing, restricted.astype(BF16))
    low_half = lax.broadcasted_iota(jnp.int32, (rows // 2, 128), 1) < 64
    for d in range(9):
        part = outgoing[d * rows : (d + 1) * rows]
        tail = jnp.concatenate([part[:, 128:values], jnp.zeros((rows, 256 - values), F32)], axis=1)
        tail = jnp.where(low_half, tail[: rows // 2], pltpu.roll(tail[rows // 2 :], 64, 1))
        if d == OWN:
            rhs_own[0:rows] = part[:, 0:128]
            rhs_own[rows:] = tail
        else:
            rhs_send[SLOT[d], 0:rows] = part[:, 0:128].astype(BF16)
            rhs_send[SLOT[d], rows:] = tail.astype(BF16)

    inverse_copy.wait()
    small[5].wait()

    def block_of(c, d, dz):
        t = d * 3 + dz + 1
        if t == 13:
            return own_v.at[c]
        return raw[c].at[inverse_s[c, t - (1 if t > 13 else 0)]]

    def repack(c):
        big[c].wait()
        if c + AHEAD < bricks:
            big[c + AHEAD].start()
        partner = 1 if c % 2 == 0 else -1
        edge = c == 0 or c == bricks - 1
        for d in range(9):
            here = block_of(c, d, 0)
            near = block_of(c, d, partner)
            packed[c, :, d * 128 : (d + 1) * 128] = here[:, 0:128]
            packed[c, :, (9 + d) * 128 : (10 + d) * 128] = jnp.concatenate(
                [here[:, 128:values], near[:, 128:values]], axis=1
            )
            packed[c, :, (18 + d) * 128 : (19 + d) * 128] = near[:, 0:128]
            if not edge:
                packed[c, :, (27 + d) * 128 : (28 + d) * 128] = block_of(c, d, -partner)[:, 0:128]
        at = 36
        if not edge:
            for d, e in JOINED:
                packed[c, :, at * 128 : (at + 1) * 128] = jnp.concatenate(
                    [
                        block_of(c, d, -partner)[:, 128:values],
                        block_of(c, e, -partner)[:, 128:values],
                    ],
                    axis=1,
                )
                at += 1
            last = block_of(c, OWN, -partner)[:, 128:values]
            packed[c, :, at * 128 : (at + 1) * 128] = jnp.concatenate(
                [last, jnp.zeros_like(last)], axis=1
            )

    for c in range(3):
        repack(c)

    pl.semaphore_wait(barrier, beside)
    to_each(
        lambda d, target: pltpu.make_async_remote_copy(
            src_ref=rhs_send.at[SLOT[d]],
            dst_ref=rhs_land.at[SLOT[8 - d]],
            send_sem=rhs_sems.at[0],
            recv_sem=rhs_sems.at[1],
            device_id=target,
            device_id_type=pl.DeviceIdType.MESH,
        ).start()
    )

    for c in range(3, 7):
        repack(c)

    square = lax.broadcasted_iota(jnp.int32, (slots, slots), 0) == lax.broadcasted_iota(
        jnp.int32, (slots, slots), 1
    )

    def upright(row):
        return jnp.sum(
            jnp.where(square, row.astype(F32), 0.0), axis=1, keepdims=True
        ).astype(jnp.int32)

    dest_up = upright(dest)
    column_id = lax.broadcasted_iota(jnp.int32, (slots, 9 * rows), 1)
    for l in range(loads):
        gather_v[l * slots : (l + 1) * slots, :] = jnp.where(
            column_id == dest_up * 8 + l, 1.0, 0.0
        ).astype(BF16)
    diagonal = lax.broadcasted_iota(jnp.int32, (values, values), 0) == lax.broadcasted_iota(
        jnp.int32, (values, values), 1
    )
    unit = jnp.where(diagonal, 1.0, 0.0).astype(BF16)
    for o in range(8):
        restrict_t[o] = dot_nt(unit, restrict_b[o]).astype(BF16)

    for p in range(pairs):
        halves = []
        for c in (2 * p, 2 * p + 1):
            found = jnp.sum(
                jnp.where(diagonal, own_v[c].astype(F32), 0.0), axis=0, keepdims=True
            )
            halves.append(jnp.broadcast_to(DAMPING / found, (8, values)))
        scale = jnp.concatenate(halves, axis=0)
        scale_v[p, :, 0:128] = scale[:, 0:128]
        scale_v[p, :, 128:256] = jnp.concatenate(
            [scale[:, 128:values], jnp.zeros((16, 256 - values), F32)], axis=1
        )

    low = lax.broadcasted_iota(jnp.int32, (16, 128), 1) < 64

    def publish(par, p, value):
        tail = value[:, 128:256]
        own[par, p, 0] = value[:, 0:128].astype(BF16)
        own[par, p, 1] = jnp.where(low, tail, pltpu.roll(swapped(tail), 64, 1)).astype(BF16)

    def send(par, q):
        to_each(
            lambda d, target: pltpu.make_async_remote_copy(
                src_ref=own.at[par, pl.ds(2 * q, 2)],
                dst_ref=land.at[par, SLOT[8 - d], pl.ds(2 * q, 2)],
                send_sem=send_sems.at[par, q],
                recv_sem=recv_sems.at[par, q],
                device_id=target,
                device_id_type=pl.DeviceIdType.MESH,
            ).start()
        )

    def wait_chunk(par, q, sems):
        wait_each(land.at[par, :, pl.ds(2 * q, 2)], sems.at[par, q])

    def column(par, d, p, kind):
        return own[par, p, kind] if d == OWN else land[par, SLOT[d], p, kind]

    wait_each(rhs_land, rhs_sems.at[1])
    for p in range(pairs):
        def rhs_rows(r):
            total = rhs_own[r : r + 16]
            for s in range(8):
                total += rhs_land[s, r : r + 16].astype(F32)
            return total

        head = rhs_rows(16 * p)
        tail = rhs_rows(rows + 16 * (p % (pairs // 2)))
        if p >= pairs // 2:
            tail = pltpu.roll(tail, 64, 1)
        rhs = jnp.concatenate([head, tail], axis=1)
        rhs_v[p] = rhs
        first = scale_v[p] * rhs
        solution_v[p] = first
        publish(0, p, first)
        if p % 2 == 1:
            send(0, p // 2)
    wait_each(rhs_send, rhs_sems.at[0])

    for c in range(7, bricks):
        repack(c)

    def expand(par, q):
        for p in (2 * q, 2 * q + 1):
            for d in range(9):
                turned[d, p] = swapped(column(par, d, p, 0).astype(F32)).astype(BF16)
            for i, (d, e) in enumerate(JOINED + ((OWN, OWN),)):
                left = column(par, d, p, 1).astype(F32)
                right = column(par, e, p, 1).astype(F32)
                joined[i, p] = jnp.where(low, pltpu.roll(left, 64, 1), right).astype(BF16)

    def apply(par, c):
        p = c // 2
        other = p - 1 if c % 2 == 0 else p + 1
        edge = c == 0 or c == bricks - 1
        tiles = [column(par, d, p, 0) for d in range(9)]
        tiles += [column(par, d, p, 1) for d in range(9)]
        tiles += [turned[d, p] for d in range(9)]
        if not edge:
            tiles += [turned[d, other] for d in range(9)]
            tiles += [joined[i, other] for i in range(5)]
        depth = 128 * len(tiles)
        return dot_nt(jnp.concatenate(tiles, axis=1), packed[c, :, 0:depth])

    def step(e, carry):
        now = lax.rem(e, 2)
        later = 1 - now

        def finish(p, even, odd):
            applied = jnp.concatenate([even[0:8], odd[8:16]], axis=0)
            applied = jnp.concatenate([applied, jnp.zeros((16, 256 - values), F32)], axis=1)
            value = solution_v[p] + scale_v[p] * (rhs_v[p] - applied)
            solution_v[p] = value
            publish(later, p, value)

        for q in range(3):
            for c in range(4 * q, 4 * q + 4):
                if c == 0:
                    wait_chunk(now, 0, recv_sems)
                    expand(now, 0)
                if c % 4 == 3 and q < 2:
                    wait_chunk(now, q + 1, recv_sems)
                    expand(now, q + 1)
                result = apply(now, c)
                if c % 2 == 0:
                    even = result
                else:
                    finish(c // 2, even, result)
            send(later, q)
            wait_chunk(now, q, send_sems)
        return carry

    lax.fori_loop(0, SWEEPS - 1, step, 0)

    end = (SWEEPS - 1) % 2
    for p in range(pairs):
        for half in range(2):
            coarse_ref[2 * p + half] = solution_v[p, 8 * half : 8 * half + loads, 0:values]
    for q in range(3):
        wait_chunk(end, q, recv_sems)
        wait_chunk(end, q, send_sems)
    around = jnp.concatenate(
        [
            jnp.concatenate([column(end, d, p, 0), column(end, d, p, 1)], axis=1)
            for d in range(9)
            for p in range(pairs)
        ],
        axis=0,
    )
    fetched = dot(gather_v[...], around)[:, 0:values].astype(BF16)
    octant_up = jnp.concatenate([upright(octant)] * loads, axis=0)
    total = jnp.zeros((values, loads * slots), F32)
    for o in range(8):
        chosen = fetched * jnp.where(octant_up == o, 1.0, 0.0).astype(BF16)
        total += dot_nt(restrict_t[o], chosen)
    for l in range(loads):
        correction_ref[l] = total[:, l * slots : (l + 1) * slots] * mask


def local(fine_list, fine_residual, solid_bits, restrict_ops, operator, pattern):
    slots, loads, values = fine_residual.shape
    bricks = operator.shape[2]
    pairs = bricks // 2
    rows = bricks * 8
    any_space = pl.BlockSpec(memory_space=pl.ANY)
    vmem = pl.BlockSpec(memory_space=pltpu.VMEM)
    dma = pltpu.SemaphoreType.DMA
    correction, coarse = pl.pallas_call(
        kernel,
        out_shape=[
            jax.ShapeDtypeStruct((loads, values, slots), F32),
            jax.ShapeDtypeStruct((bricks, loads, values), F32),
        ],
        in_specs=[any_space] * 6,
        out_specs=[vmem, vmem],
        scratch_shapes=[
            pltpu.VMEM((1, slots), jnp.int32),
            pltpu.VMEM((3, slots), jnp.int32),
            pltpu.VMEM((loads, values, slots), F32),
            pltpu.VMEM((8, values, values), F32),
            pltpu.VMEM((bricks, values, values), BF16),
            pltpu.VMEM((bricks, 1, 26), jnp.int32),
            pltpu.VMEM((16, 128), jnp.int32),
            pltpu.SMEM((16, 128), jnp.int32),
            pltpu.VMEM((bricks, values, 41 * 128), BF16),
            pltpu.VMEM((8, values, values), BF16),
            pltpu.VMEM((8, values, values), BF16),
            pltpu.VMEM((loads * slots, 9 * rows), BF16),
            pltpu.VMEM((rows * 3 // 2, 128), F32),
            pltpu.VMEM((8, rows * 3 // 2, 128), BF16),
            pltpu.VMEM((8, rows * 3 // 2, 128), BF16),
            pltpu.VMEM((2, 8, pairs, 2, 16, 128), BF16),
            pltpu.VMEM((2, pairs, 2, 16, 128), BF16),
            pltpu.VMEM((9, pairs, 16, 128), BF16),
            pltpu.VMEM((5, pairs, 16, 128), BF16),
            pltpu.VMEM((pairs, 16, 256), F32),
            pltpu.VMEM((pairs, 16, 256), F32),
            pltpu.VMEM((pairs, 16, 256), F32),
            dma((6,)),
            dma((bricks,)),
            dma,
            dma((2,)),
            dma((2, 3)),
            dma((2, 3)),
        ]
        + [pltpu.VMEM((26, values, values), BF16)] * bricks,
        compiler_params=pltpu.CompilerParams(
            collective_id=0, has_side_effects=True, vmem_limit_bytes=63 * 2**20
        ),
    )(
        fine_list.reshape(1, slots),
        solid_bits.T,
        fine_residual.transpose(1, 2, 0),
        restrict_ops,
        operator.reshape(bricks, 27, values, values),
        pattern.reshape(bricks, 1, 26),
    )
    return correction.transpose(2, 0, 1), coarse.reshape(1, 1, bricks, loads, values)


def solution(mesh):
    in_specs = (
        P(("gx", "gy")),
        P(("gx", "gy"), None, None),
        P(("gx", "gy"), None),
        P(),
        P("gx", "gy", None, None, None, None),
        P("gx", "gy", None, None),
    )
    out_specs = (P(("gx", "gy"), None, None), P("gx", "gy", None, None, None))
    return jax.shard_map(local, mesh=mesh, in_specs=in_specs, out_specs=out_specs, check_vma=False)
```

```python
import functools
import jax
import jax.numpy as jnp
from jax import lax
from jax.experimental import pallas as pl
from jax.experimental.pallas import tpu as pltpu
from jax.sharding import PartitionSpec as P

SWEEPS = 8
DAMPING = 0.8
OFFSETS = [(dx, dy) for dx in (-1, 0, 1) for dy in (-1, 0, 1)]
OWN = 4
NEIGHBOURS = [d for d in range(9) if d != OWN]
ARRIVE = (0, 3, 7)
LEAVE = (3, 7, 11)
AHEAD = 4
SLOT = {d: (d if d < OWN else d - 1) for d in range(9) if d != OWN}
JOINED = ((0, 1), (2, 3), (5, 6), (7, 8))
NT = (((1,), (1,)), ((), ()))
F32 = jnp.float32
BF16 = jnp.bfloat16


def dot(a, b):
    return jnp.dot(a, b, preferred_element_type=F32)


def dot_nt(a, b):
    return lax.dot_general(a, b, NT, preferred_element_type=F32)


def swapped(tile):
    return jnp.concatenate([tile[8:16], tile[0:8]], axis=0)


def kernel(
    list_hbm, bits_hbm, residual_hbm, restrict_hbm, operator_hbm, pattern_hbm,
    correction_ref, coarse_ref,
    list_v, bits_v, residual_v, restrict_v, own_v, pattern_v, inverse_v, inverse_s,
    packed, restrict_b, restrict_t, gather_v, rhs_own, rhs_send, rhs_land,
    land, own, turned, joined, applied_v, solution_v, rhs_v, scale_v,
    small_sem, raw_sem, inverse_sem, rhs_sems, send_sems, recv_sems,
    *raw,
):
    bricks = len(raw)
    pairs = bricks // 2
    loads = residual_v.shape[0]
    values = restrict_v.shape[1]
    slots = list_v.shape[1]
    rows = bricks * 8
    count_x = lax.axis_size("gx")
    count_y = lax.axis_size("gy")
    here_x = lax.axis_index("gx")
    here_y = lax.axis_index("gy")

    small = [
        pltpu.make_async_copy(src, dst, small_sem.at[i])
        for i, (src, dst) in enumerate(
            [
                (pattern_hbm, pattern_v),
                (list_hbm, list_v),
                (bits_hbm, bits_v),
                (residual_hbm, residual_v),
                (restrict_hbm, restrict_v),
                (operator_hbm.at[:, 0], own_v),
            ]
        )
    ]
    for copy in small:
        copy.start()
    big = [
        pltpu.make_async_copy(operator_hbm.at[c, pl.ds(1, 26)], raw[c], raw_sem.at[c])
        for c in range(bricks)
    ]

    land[...] = jnp.zeros(land.shape, BF16)
    rhs_land[...] = jnp.zeros(rhs_land.shape, BF16)

    applied_v[...] = jnp.zeros(applied_v.shape, F32)

    inside = {}
    around_x = 3 - (here_x == 0).astype(jnp.int32) - (here_x == count_x - 1).astype(jnp.int32)
    around_y = 3 - (here_y == 0).astype(jnp.int32) - (here_y == count_y - 1).astype(jnp.int32)
    beside = around_x * around_y - 1
    for d, (dx, dy) in enumerate(OFFSETS):
        to_x = here_x + dx
        to_y = here_y + dy
        if d != OWN:
            inside[d] = (to_x >= 0) & (to_x < count_x) & (to_y >= 0) & (to_y < count_y)

    def to_each(action):
        for d in (0, 2, 6, 8, 3, 5, 1, 7):
            dx, dy = OFFSETS[d]

            @pl.when(inside[d])
            def _():
                action(d, (here_x + dx, here_y + dy))

    def wait_each(part, sem):
        for count in (8, 5, 3):

            @pl.when(beside == count)
            def _():
                some = part.at[pl.ds(0, count)]
                pltpu.make_async_copy(some, some, sem).wait()

    barrier = pltpu.get_barrier_semaphore()
    to_each(
        lambda d, target: pl.semaphore_signal(
            barrier, inc=1, device_id=target, device_id_type=pl.DeviceIdType.MESH
        )
    )

    small[0].wait()
    pattern = pattern_v[...].reshape(bricks, 26)
    lane = lax.broadcasted_iota(jnp.int32, (bricks, 26), 1)
    wide = lax.broadcasted_iota(jnp.int32, (bricks, 128), 1)
    inverse = jnp.zeros((bricks, 128), jnp.int32)
    for t in range(26):
        at = jnp.max(jnp.where(pattern == t, lane, 0), axis=1, keepdims=True)
        inverse = jnp.where(wide == t, at, inverse)
    inverse_v[...] = jnp.zeros(inverse_v.shape, jnp.int32)
    inverse_v[0:bricks] = inverse
    inverse_copy = pltpu.make_async_copy(inverse_v, inverse_s, inverse_sem)
    inverse_copy.start()

    small[1].wait()
    small[2].wait()
    entry = list_v[...]
    live = entry >= 0
    brick = entry >> 3
    octant = jnp.where(live, entry & 7, -1)
    line = (brick * 43691) >> 19
    pos_z = brick - line * bricks
    step_x = (line >> 4) - here_x
    step_y = (line & 15) - here_y
    dest = ((step_x + 1) * 3 + step_y + 1) * bricks + pos_z
    dest = jnp.where(live, dest, -8)

    node = lax.broadcasted_iota(jnp.int32, (values // 3, slots), 0)
    word = jnp.where(
        node < 30, bits_v[0:1, :], jnp.where(node < 60, bits_v[1:2, :], bits_v[2:3, :])
    )
    shift = node - jnp.where(node >= 30, 30, 0) - jnp.where(node >= 60, 30, 0)
    flags = (lax.shift_right_logical(word, shift) & 1).astype(F32)
    flags = jnp.where(live, flags, 0.0)
    mask = jnp.concatenate([flags, flags, flags], axis=0)

    small[3].wait()
    masked = jnp.concatenate(
        [(residual_v[l] * mask).astype(BF16) for l in range(loads)], axis=1
    )
    small[4].wait()
    for c in range(AHEAD):
        big[c].start()
    octants = jnp.concatenate([octant] * loads, axis=1)
    restricted = jnp.zeros((values, loads * slots), F32)
    for o in range(8):
        matrix = restrict_v[o].astype(BF16)
        restrict_b[o] = matrix
        chosen = masked * jnp.where(octants == o, 1.0, 0.0).astype(BF16)
        restricted += dot(matrix, chosen)
    key = jnp.concatenate([dest * 8 + l for l in range(loads)], axis=1)
    row_id = lax.broadcasted_iota(jnp.int32, (9 * rows, loads * slots), 0)
    summing = jnp.where(row_id == key, 1.0, 0.0).astype(BF16)
    outgoing = dot_nt(summing, restricted.astype(BF16))
    low_half = lax.broadcasted_iota(jnp.int32, (rows // 2, 128), 1) < 64
    for d in range(9):
        part = outgoing[d * rows : (d + 1) * rows]
        tail = jnp.concatenate([part[:, 128:values], jnp.zeros((rows, 256 - values), F32)], axis=1)
        tail = jnp.where(low_half, tail[: rows // 2], pltpu.roll(tail[rows // 2 :], 64, 1))
        if d == OWN:
            rhs_own[0:rows] = part[:, 0:128]
            rhs_own[rows:] = tail
        else:
            rhs_send[SLOT[d], 0:rows] = part[:, 0:128].astype(BF16)
            rhs_send[SLOT[d], rows:] = tail.astype(BF16)

    inverse_copy.wait()
    small[5].wait()

    def block_of(c, d, dz):
        t = d * 3 + dz + 1
        if t == 13:
            return own_v.at[c]
        return raw[c].at[inverse_s[c, t - (1 if t > 13 else 0)]]

    def repack(c):
        big[c].wait()
        if c + AHEAD < bricks:
            big[c + AHEAD].start()
        partner = 1 if c % 2 == 0 else -1
        edge = c == 0 or c == bricks - 1

        def put(at, value):
            packed[c, :, at * 128 : (at + 1) * 128] = value

        def halves(left, right):
            return jnp.concatenate([left[:, 128:values], right[:, 128:values]], axis=1)

        at = 0
        here = block_of(c, OWN, 0)
        near = block_of(c, OWN, partner)
        put(0, here[:, 0:128])
        put(1, halves(here, near))
        put(2, near[:, 0:128])
        at = 3
        if not edge:
            far = block_of(c, OWN, -partner)
            put(3, far[:, 0:128])
            last = far[:, 128:values]
            put(4, jnp.concatenate([last, jnp.zeros_like(last)], axis=1))
            at = 5
        for i, d in enumerate(NEIGHBOURS):
            here = block_of(c, d, 0)
            near = block_of(c, d, partner)
            put(at + i, here[:, 0:128])
            put(at + 8 + i, halves(here, near))
            put(at + 16 + i, near[:, 0:128])
            if not edge:
                put(at + 24 + i, block_of(c, d, -partner)[:, 0:128])
        if not edge:
            for i, (d, e) in enumerate(JOINED):
                put(at + 32 + i, halves(block_of(c, d, -partner), block_of(c, e, -partner)))

    for c in range(3):
        repack(c)

    pl.semaphore_wait(barrier, beside)
    to_each(
        lambda d, target: pltpu.make_async_remote_copy(
            src_ref=rhs_send.at[SLOT[d]],
            dst_ref=rhs_land.at[SLOT[8 - d]],
            send_sem=rhs_sems.at[0],
            recv_sem=rhs_sems.at[1],
            device_id=target,
            device_id_type=pl.DeviceIdType.MESH,
        ).start()
    )

    for c in range(3, 7):
        repack(c)

    square = lax.broadcasted_iota(jnp.int32, (slots, slots), 0) == lax.broadcasted_iota(
        jnp.int32, (slots, slots), 1
    )

    def upright(row):
        return jnp.sum(
            jnp.where(square, row.astype(F32), 0.0), axis=1, keepdims=True
        ).astype(jnp.int32)

    dest_up = upright(dest)
    column_id = lax.broadcasted_iota(jnp.int32, (slots, 9 * rows), 1)
    for l in range(loads):
        gather_v[l * slots : (l + 1) * slots, :] = jnp.where(
            column_id == dest_up * 8 + l, 1.0, 0.0
        ).astype(BF16)
    diagonal = lax.broadcasted_iota(jnp.int32, (values, values), 0) == lax.broadcasted_iota(
        jnp.int32, (values, values), 1
    )
    unit = jnp.where(diagonal, 1.0, 0.0).astype(BF16)
    for o in range(8):
        restrict_t[o] = dot_nt(unit, restrict_b[o]).astype(BF16)

    for p in range(pairs):
        halves = []
        for c in (2 * p, 2 * p + 1):
            found = jnp.sum(
                jnp.where(diagonal, own_v[c].astype(F32), 0.0), axis=0, keepdims=True
            )
            halves.append(jnp.broadcast_to(DAMPING / found, (8, values)))
        scale = jnp.concatenate(halves, axis=0)
        scale_v[p, :, 0:128] = scale[:, 0:128]
        scale_v[p, :, 128:256] = jnp.concatenate(
            [scale[:, 128:values], jnp.zeros((16, 256 - values), F32)], axis=1
        )

    low = lax.broadcasted_iota(jnp.int32, (16, 128), 1) < 64

    def publish(par, p, value):
        tail = value[:, 128:256]
        own[par, p, 0] = value[:, 0:128].astype(BF16)
        own[par, p, 1] = jnp.where(low, tail, pltpu.roll(swapped(tail), 64, 1)).astype(BF16)
        turned[OWN, p] = swapped(value[:, 0:128]).astype(BF16)
        joined[len(JOINED), p] = swapped(tail).astype(BF16)

    def send(par, q):
        to_each(
            lambda d, target: pltpu.make_async_remote_copy(
                src_ref=own.at[par, pl.ds(2 * q, 2)],
                dst_ref=land.at[par, SLOT[8 - d], pl.ds(2 * q, 2)],
                send_sem=send_sems.at[par, q],
                recv_sem=recv_sems.at[par, q],
                device_id=target,
                device_id_type=pl.DeviceIdType.MESH,
            ).start()
        )

    def wait_chunk(par, q, sems):
        wait_each(land.at[par, :, pl.ds(2 * q, 2)], sems.at[par, q])

    def column(par, d, p, kind):
        return own[par, p, kind] if d == OWN else land[par, SLOT[d], p, kind]

    wait_each(rhs_land, rhs_sems.at[1])
    for p in range(pairs):
        def rhs_rows(r):
            total = rhs_own[r : r + 16]
            for s in range(8):
                total += rhs_land[s, r : r + 16].astype(F32)
            return total

        head = rhs_rows(16 * p)
        tail = rhs_rows(rows + 16 * (p % (pairs // 2)))
        if p >= pairs // 2:
            tail = pltpu.roll(tail, 64, 1)
        rhs = jnp.concatenate([head, tail], axis=1)
        rhs_v[p] = rhs
        first = scale_v[p] * rhs
        solution_v[p] = first
        publish(0, p, first)
        if p % 2 == 1:
            send(0, p // 2)
    wait_each(rhs_send, rhs_sems.at[0])

    for c in range(7, bricks):
        repack(c)

    def expand(par, q):
        for p in (2 * q, 2 * q + 1):
            for d in NEIGHBOURS:
                turned[d, p] = swapped(land[par, SLOT[d], p, 0].astype(F32)).astype(BF16)
            for i, (d, e) in enumerate(JOINED):
                left = land[par, SLOT[d], p, 1].astype(F32)
                right = land[par, SLOT[e], p, 1].astype(F32)
                joined[i, p] = jnp.where(low, pltpu.roll(left, 64, 1), right).astype(BF16)

    def apply(par, c, columns, pairs_joined, at):
        p = c // 2
        other = p - 1 if c % 2 == 0 else p + 1
        tiles = [column(par, d, p, 0) for d in columns]
        tiles += [column(par, d, p, 1) for d in columns]
        tiles += [turned[d, p] for d in columns]
        if c != 0 and c != bricks - 1:
            tiles += [turned[d, other] for d in columns]
            tiles += [joined[i, other] for i in pairs_joined]
        depth = 128 * len(tiles)
        return dot_nt(jnp.concatenate(tiles, axis=1), packed[c, :, at : at + depth])

    def apply_own(par, c):
        return apply(par, c, [OWN], [len(JOINED)], 0)

    def apply_neighbours(par, c):
        at = 3 if c == 0 or c == bricks - 1 else 5
        return apply(par, c, NEIGHBOURS, range(len(JOINED)), 128 * at)

    def step(e, carry):
        now = lax.rem(e, 2)
        later = 1 - now

        def keep(c, result, add):
            part = slice(0, 8) if c % 2 == 0 else slice(8, 16)
            for lanes in (slice(0, 128), slice(128, values)):
                kept = result[part, lanes]
                if add:
                    kept += applied_v[c // 2, part, lanes]
                applied_v[c // 2, part, lanes] = kept

        def finish(p):
            value = solution_v[p] + scale_v[p] * (rhs_v[p] - applied_v[p])
            solution_v[p] = value
            publish(later, p, value)

        for c in range(bricks):
            keep(c, apply_own(now, c), False)
        for c in range(bricks):
            if c in ARRIVE:
                q = ARRIVE.index(c)
                wait_chunk(now, q, recv_sems)
                expand(now, q)
            keep(c, apply_neighbours(now, c), True)
            if c % 2 == 1:
                finish(c // 2)
            if c in LEAVE:
                q = LEAVE.index(c)
                send(later, q)
                wait_chunk(now, q, send_sems)
        return carry

    lax.fori_loop(0, SWEEPS - 1, step, 0)

    end = (SWEEPS - 1) % 2
    for p in range(pairs):
        for half in range(2):
            coarse_ref[2 * p + half] = solution_v[p, 8 * half : 8 * half + loads, 0:values]
    for q in range(3):
        wait_chunk(end, q, recv_sems)
        wait_chunk(end, q, send_sems)
    around = jnp.concatenate(
        [
            jnp.concatenate([column(end, d, p, 0), column(end, d, p, 1)], axis=1)
            for d in range(9)
            for p in range(pairs)
        ],
        axis=0,
    )
    fetched = dot(gather_v[...], around)[:, 0:values].astype(BF16)
    octant_up = jnp.concatenate([upright(octant)] * loads, axis=0)
    total = jnp.zeros((values, loads * slots), F32)
    for o in range(8):
        chosen = fetched * jnp.where(octant_up == o, 1.0, 0.0).astype(BF16)
        total += dot_nt(restrict_t[o], chosen)
    for l in range(loads):
        correction_ref[l] = total[:, l * slots : (l + 1) * slots] * mask


def local(fine_list, fine_residual, solid_bits, restrict_ops, operator, pattern):
    slots, loads, values = fine_residual.shape
    bricks = operator.shape[2]
    pairs = bricks // 2
    rows = bricks * 8
    any_space = pl.BlockSpec(memory_space=pl.ANY)
    vmem = pl.BlockSpec(memory_space=pltpu.VMEM)
    dma = pltpu.SemaphoreType.DMA
    correction, coarse = pl.pallas_call(
        kernel,
        out_shape=[
            jax.ShapeDtypeStruct((loads, values, slots), F32),
            jax.ShapeDtypeStruct((bricks, loads, values), F32),
        ],
        in_specs=[any_space] * 6,
        out_specs=[vmem, vmem],
        scratch_shapes=[
            pltpu.VMEM((1, slots), jnp.int32),
            pltpu.VMEM((3, slots), jnp.int32),
            pltpu.VMEM((loads, values, slots), F32),
            pltpu.VMEM((8, values, values), F32),
            pltpu.VMEM((bricks, values, values), BF16),
            pltpu.VMEM((bricks, 1, 26), jnp.int32),
            pltpu.VMEM((16, 128), jnp.int32),
            pltpu.SMEM((16, 128), jnp.int32),
            pltpu.VMEM((bricks, values, 41 * 128), BF16),
            pltpu.VMEM((8, values, values), BF16),
            pltpu.VMEM((8, values, values), BF16),
            pltpu.VMEM((loads * slots, 9 * rows), BF16),
            pltpu.VMEM((rows * 3 // 2, 128), F32),
            pltpu.VMEM((8, rows * 3 // 2, 128), BF16),
            pltpu.VMEM((8, rows * 3 // 2, 128), BF16),
            pltpu.VMEM((2, 8, pairs, 2, 16, 128), BF16),
            pltpu.VMEM((2, pairs, 2, 16, 128), BF16),
            pltpu.VMEM((9, pairs, 16, 128), BF16),
            pltpu.VMEM((5, pairs, 16, 128), BF16),
            pltpu.VMEM((pairs, 16, 256), F32),
            pltpu.VMEM((pairs, 16, 256), F32),
            pltpu.VMEM((pairs, 16, 256), F32),
            pltpu.VMEM((pairs, 16, 256), F32),
            dma((6,)),
            dma((bricks,)),
            dma,
            dma((2,)),
            dma((2, 3)),
            dma((2, 3)),
        ]
        + [pltpu.VMEM((26, values, values), BF16)] * bricks,
        compiler_params=pltpu.CompilerParams(
            collective_id=0, has_side_effects=True, vmem_limit_bytes=63 * 2**20
        ),
    )(
        fine_list.reshape(1, slots),
        solid_bits.T,
        fine_residual.transpose(1, 2, 0),
        restrict_ops,
        operator.reshape(bricks, 27, values, values),
        pattern.reshape(bricks, 1, 26),
    )
    return correction.transpose(2, 0, 1), coarse.reshape(1, 1, bricks, loads, values)


def solution(mesh):
    in_specs = (
        P(("gx", "gy")),
        P(("gx", "gy"), None, None),
        P(("gx", "gy"), None),
        P(),
        P("gx", "gy", None, None, None, None),
        P("gx", "gy", None, None),
    )
    out_specs = (P(("gx", "gy"), None, None), P("gx", "gy", None, None, None))
    return jax.shard_map(local, mesh=mesh, in_specs=in_specs, out_specs=out_specs, check_vma=False)
```

```python
import functools
import jax
import jax.numpy as jnp
from jax import lax
from jax.experimental import pallas as pl
from jax.experimental.pallas import tpu as pltpu
from jax.sharding import PartitionSpec as P

SWEEPS = 8
DAMPING = 0.8
OFFSETS = [(dx, dy) for dx in (-1, 0, 1) for dy in (-1, 0, 1)]
OWN = 4
NEIGHBOURS = [d for d in range(9) if d != OWN]
ARRIVE = (0, 3, 7)
LEAVE = (4, 7, 11)
AHEAD = 4
SLOT = {d: (d if d < OWN else d - 1) for d in range(9) if d != OWN}
JOINED = ((0, 1), (2, 3), (5, 6), (7, 8))
NT = (((1,), (1,)), ((), ()))
F32 = jnp.float32
BF16 = jnp.bfloat16


def dot(a, b):
    return jnp.dot(a, b, preferred_element_type=F32)


def dot_nt(a, b):
    return lax.dot_general(a, b, NT, preferred_element_type=F32)


def swapped(tile):
    return jnp.concatenate([tile[8:16], tile[0:8]], axis=0)


def kernel(
    list_hbm, bits_hbm, residual_hbm, restrict_hbm, operator_hbm, pattern_hbm,
    correction_ref, coarse_ref,
    list_v, bits_v, residual_v, restrict_v, own_v, pattern_v, inverse_v, inverse_s,
    packed, restrict_b, restrict_t, gather_v, rhs_own, rhs_send, rhs_land,
    land, own, turned, joined, applied_v, solution_v, rhs_v, scale_v,
    small_sem, raw_sem, inverse_sem, rhs_sems, send_sems, recv_sems,
    *raw,
):
    bricks = len(raw)
    pairs = bricks // 2
    loads = residual_v.shape[0]
    values = restrict_v.shape[1]
    slots = list_v.shape[1]
    rows = bricks * 8
    count_x = lax.axis_size("gx")
    count_y = lax.axis_size("gy")
    here_x = lax.axis_index("gx")
    here_y = lax.axis_index("gy")

    small = [
        pltpu.make_async_copy(src, dst, small_sem.at[i])
        for i, (src, dst) in enumerate(
            [
                (pattern_hbm, pattern_v),
                (list_hbm, list_v),
                (bits_hbm, bits_v),
                (residual_hbm, residual_v),
                (restrict_hbm, restrict_v),
                (operator_hbm.at[:, 0], own_v),
            ]
        )
    ]
    for copy in small:
        copy.start()
    big = [
        pltpu.make_async_copy(operator_hbm.at[c, pl.ds(1, 26)], raw[c], raw_sem.at[c])
        for c in range(bricks)
    ]

    land[...] = jnp.zeros(land.shape, BF16)
    rhs_land[...] = jnp.zeros(rhs_land.shape, BF16)

    applied_v[...] = jnp.zeros(applied_v.shape, F32)

    inside = {}
    around_x = 3 - (here_x == 0).astype(jnp.int32) - (here_x == count_x - 1).astype(jnp.int32)
    around_y = 3 - (here_y == 0).astype(jnp.int32) - (here_y == count_y - 1).astype(jnp.int32)
    beside = around_x * around_y - 1
    for d, (dx, dy) in enumerate(OFFSETS):
        to_x = here_x + dx
        to_y = here_y + dy
        if d != OWN:
            inside[d] = (to_x >= 0) & (to_x < count_x) & (to_y >= 0) & (to_y < count_y)

    def to_each(action):
        for d in (0, 2, 6, 8, 3, 5, 1, 7):
            dx, dy = OFFSETS[d]

            @pl.when(inside[d])
            def _():
                action(d, (here_x + dx, here_y + dy))

    def wait_each(part, sem):
        for count in (8, 5, 3):

            @pl.when(beside == count)
            def _():
                some = part.at[pl.ds(0, count)]
                pltpu.make_async_copy(some, some, sem).wait()

    barrier = pltpu.get_barrier_semaphore()
    to_each(
        lambda d, target: pl.semaphore_signal(
            barrier, inc=1, device_id=target, device_id_type=pl.DeviceIdType.MESH
        )
    )

    small[0].wait()
    pattern = pattern_v[...].reshape(bricks, 26)
    lane = lax.broadcasted_iota(jnp.int32, (bricks, 26), 1)
    wide = lax.broadcasted_iota(jnp.int32, (bricks, 128), 1)
    inverse = jnp.zeros((bricks, 128), jnp.int32)
    for t in range(26):
        at = jnp.max(jnp.where(pattern == t, lane, 0), axis=1, keepdims=True)
        inverse = jnp.where(wide == t, at, inverse)
    inverse_v[...] = jnp.zeros(inverse_v.shape, jnp.int32)
    inverse_v[0:bricks] = inverse
    inverse_copy = pltpu.make_async_copy(inverse_v, inverse_s, inverse_sem)
    inverse_copy.start()

    small[1].wait()
    small[2].wait()
    entry = list_v[...]
    live = entry >= 0
    brick = entry >> 3
    octant = jnp.where(live, entry & 7, -1)
    line = (brick * 43691) >> 19
    pos_z = brick - line * bricks
    step_x = (line >> 4) - here_x
    step_y = (line & 15) - here_y
    dest = ((step_x + 1) * 3 + step_y + 1) * bricks + pos_z
    dest = jnp.where(live, dest, -8)

    node = lax.broadcasted_iota(jnp.int32, (values // 3, slots), 0)
    word = jnp.where(
        node < 30, bits_v[0:1, :], jnp.where(node < 60, bits_v[1:2, :], bits_v[2:3, :])
    )
    shift = node - jnp.where(node >= 30, 30, 0) - jnp.where(node >= 60, 30, 0)
    flags = (lax.shift_right_logical(word, shift) & 1).astype(F32)
    flags = jnp.where(live, flags, 0.0)
    mask = jnp.concatenate([flags, flags, flags], axis=0)

    small[3].wait()
    masked = jnp.concatenate(
        [(residual_v[l] * mask).astype(BF16) for l in range(loads)], axis=1
    )
    small[4].wait()
    for c in range(AHEAD):
        big[c].start()
    octants = jnp.concatenate([octant] * loads, axis=1)
    restricted = jnp.zeros((values, loads * slots), F32)
    for o in range(8):
        matrix = restrict_v[o].astype(BF16)
        restrict_b[o] = matrix
        chosen = masked * jnp.where(octants == o, 1.0, 0.0).astype(BF16)
        restricted += dot(matrix, chosen)
    key = jnp.concatenate([dest * 8 + l for l in range(loads)], axis=1)
    row_id = lax.broadcasted_iota(jnp.int32, (9 * rows, loads * slots), 0)
    summing = jnp.where(row_id == key, 1.0, 0.0).astype(BF16)
    outgoing = dot_nt(summing, restricted.astype(BF16))
    low = lax.broadcasted_iota(jnp.int32, (16, 128), 1) < 64
    for d in range(9):
        for q in range(3):
            at = d * rows + 32 * q
            part = outgoing[at : at + 32]
            tail = jnp.concatenate([part[:, 128:values], jnp.zeros((32, 256 - values), F32)], axis=1)
            tail = jnp.where(low, tail[0:16], pltpu.roll(tail[16:32], 64, 1))
            if d == OWN:
                rhs_own[q, 0:32] = part[:, 0:128]
                rhs_own[q, 32:48] = tail
            else:
                rhs_send[SLOT[d], q, 0:32] = part[:, 0:128].astype(BF16)
                rhs_send[SLOT[d], q, 32:48] = tail.astype(BF16)

    inverse_copy.wait()
    small[5].wait()

    def block_of(c, d, dz):
        t = d * 3 + dz + 1
        if t == 13:
            return own_v.at[c]
        return raw[c].at[inverse_s[c, t - (1 if t > 13 else 0)]]

    def repack(c):
        big[c].wait()
        if c + AHEAD < bricks:
            big[c + AHEAD].start()
        partner = 1 if c % 2 == 0 else -1
        edge = c == 0 or c == bricks - 1

        def put(at, value):
            packed[c, :, at * 128 : (at + 1) * 128] = value

        def halves(left, right):
            return jnp.concatenate([left[:, 128:values], right[:, 128:values]], axis=1)

        at = 0
        here = block_of(c, OWN, 0)
        near = block_of(c, OWN, partner)
        put(0, here[:, 0:128])
        put(1, halves(here, near))
        put(2, near[:, 0:128])
        at = 3
        if not edge:
            far = block_of(c, OWN, -partner)
            put(3, far[:, 0:128])
            last = far[:, 128:values]
            put(4, jnp.concatenate([last, jnp.zeros_like(last)], axis=1))
            at = 5
        for i, d in enumerate(NEIGHBOURS):
            here = block_of(c, d, 0)
            near = block_of(c, d, partner)
            put(at + i, here[:, 0:128])
            put(at + 8 + i, halves(here, near))
            put(at + 16 + i, near[:, 0:128])
            if not edge:
                put(at + 24 + i, block_of(c, d, -partner)[:, 0:128])
        if not edge:
            for i, (d, e) in enumerate(JOINED):
                put(at + 32 + i, halves(block_of(c, d, -partner), block_of(c, e, -partner)))

    for c in range(3):
        repack(c)

    pl.semaphore_wait(barrier, beside)
    for q in range(3):
        to_each(
            lambda d, target, q=q: pltpu.make_async_remote_copy(
                src_ref=rhs_send.at[SLOT[d], q],
                dst_ref=rhs_land.at[SLOT[8 - d], q],
                send_sem=rhs_sems.at[0, q],
                recv_sem=rhs_sems.at[1, q],
                device_id=target,
                device_id_type=pl.DeviceIdType.MESH,
            ).start()
        )

    for c in range(3, 7):
        repack(c)

    square = lax.broadcasted_iota(jnp.int32, (slots, slots), 0) == lax.broadcasted_iota(
        jnp.int32, (slots, slots), 1
    )

    def upright(row):
        return jnp.sum(
            jnp.where(square, row.astype(F32), 0.0), axis=1, keepdims=True
        ).astype(jnp.int32)

    dest_up = upright(dest)
    column_id = lax.broadcasted_iota(jnp.int32, (slots, 9 * rows), 1)
    for l in range(loads):
        gather_v[l * slots : (l + 1) * slots, :] = jnp.where(
            column_id == dest_up * 8 + l, 1.0, 0.0
        ).astype(BF16)
    diagonal = lax.broadcasted_iota(jnp.int32, (values, values), 0) == lax.broadcasted_iota(
        jnp.int32, (values, values), 1
    )
    unit = jnp.where(diagonal, 1.0, 0.0).astype(BF16)
    for o in range(8):
        restrict_t[o] = dot_nt(unit, restrict_b[o]).astype(BF16)

    for p in range(pairs):
        halves = []
        for c in (2 * p, 2 * p + 1):
            found = jnp.sum(
                jnp.where(diagonal, own_v[c].astype(F32), 0.0), axis=0, keepdims=True
            )
            halves.append(jnp.broadcast_to(DAMPING / found, (8, values)))
        scale = jnp.concatenate(halves, axis=0)
        scale_v[p, :, 0:128] = scale[:, 0:128]
        scale_v[p, :, 128:256] = jnp.concatenate(
            [scale[:, 128:values], jnp.zeros((16, 256 - values), F32)], axis=1
        )

    def publish(par, p, value):
        tail = value[:, 128:256]
        own[par, p, 0] = value[:, 0:128].astype(BF16)
        own[par, p, 1] = jnp.where(low, tail, pltpu.roll(swapped(tail), 64, 1)).astype(BF16)
        turned[OWN, p] = swapped(value[:, 0:128]).astype(BF16)
        joined[len(JOINED), p] = swapped(tail).astype(BF16)

    def send(par, q):
        to_each(
            lambda d, target: pltpu.make_async_remote_copy(
                src_ref=own.at[par, pl.ds(2 * q, 2)],
                dst_ref=land.at[par, SLOT[8 - d], pl.ds(2 * q, 2)],
                send_sem=send_sems.at[par, q],
                recv_sem=recv_sems.at[par, q],
                device_id=target,
                device_id_type=pl.DeviceIdType.MESH,
            ).start()
        )

    def wait_chunk(par, q, sems):
        wait_each(land.at[par, :, pl.ds(2 * q, 2)], sems.at[par, q])

    def column(par, d, p, kind):
        return own[par, p, kind] if d == OWN else land[par, SLOT[d], p, kind]

    for q in range(3):
        wait_each(rhs_land.at[:, q], rhs_sems.at[1, q])
        total = rhs_own[q]
        for s in range(8):
            total += rhs_land[s, q].astype(F32)
        tails = (total[32:48], pltpu.roll(total[32:48], 64, 1))
        for half in range(2):
            p = 2 * q + half
            rhs = jnp.concatenate([total[16 * half : 16 * half + 16], tails[half]], axis=1)
            rhs_v[p] = rhs
            first = scale_v[p] * rhs
            solution_v[p] = first
            publish(0, p, first)
        send(0, q)
    for q in range(3):
        wait_each(rhs_send.at[:, q], rhs_sems.at[0, q])

    for c in range(7, bricks):
        repack(c)

    def expand(par, q):
        for p in (2 * q, 2 * q + 1):
            for d in NEIGHBOURS:
                turned[d, p] = swapped(land[par, SLOT[d], p, 0].astype(F32)).astype(BF16)
            for i, (d, e) in enumerate(JOINED):
                left = land[par, SLOT[d], p, 1].astype(F32)
                right = land[par, SLOT[e], p, 1].astype(F32)
                joined[i, p] = jnp.where(low, pltpu.roll(left, 64, 1), right).astype(BF16)

    def inner_tiles(par, c, columns):
        p = c // 2
        tiles = [column(par, d, p, 0) for d in columns]
        tiles += [column(par, d, p, 1) for d in columns]
        return tiles + [turned[d, p] for d in columns]

    def outer_tiles(c, columns, pairs_joined):
        if c == 0 or c == bricks - 1:
            return []
        other = c // 2 - 1 if c % 2 == 0 else c // 2 + 1
        return [turned[d, other] for d in columns] + [joined[i, other] for i in pairs_joined]

    def multiply(c, at, tiles):
        depth = 128 * len(tiles)
        return dot_nt(jnp.concatenate(tiles, axis=1), packed[c, :, 128 * at : 128 * at + depth])

    def apply_own(par, c):
        return multiply(c, 0, inner_tiles(par, c, [OWN]) + outer_tiles(c, [OWN], [len(JOINED)]))

    def neighbours_at(c):
        return 3 if c == 0 or c == bricks - 1 else 5

    def apply_inner(par, c):
        return multiply(c, neighbours_at(c), inner_tiles(par, c, NEIGHBOURS))

    def apply_outer(c):
        return multiply(c, neighbours_at(c) + 24, outer_tiles(c, NEIGHBOURS, range(len(JOINED))))

    def apply_neighbours(par, c):
        tiles = inner_tiles(par, c, NEIGHBOURS) + outer_tiles(c, NEIGHBOURS, range(len(JOINED)))
        return multiply(c, neighbours_at(c), tiles)

    def step(e, carry):
        now = lax.rem(e, 2)
        later = 1 - now

        def keep(c, result, add):
            part = slice(0, 8) if c % 2 == 0 else slice(8, 16)
            for lanes in (slice(0, 128), slice(128, values)):
                kept = result[part, lanes]
                if add:
                    kept += applied_v[c // 2, part, lanes]
                applied_v[c // 2, part, lanes] = kept

        def finish(p):
            value = solution_v[p] + scale_v[p] * (rhs_v[p] - applied_v[p])
            solution_v[p] = value
            publish(later, p, value)

        for c in range(bricks):
            keep(c, apply_own(now, c), False)
        for c in range(bricks):
            if c in ARRIVE:
                q = ARRIVE.index(c)
                if q > 0:
                    keep(c, apply_inner(now, c), True)
                wait_chunk(now, q, recv_sems)
                expand(now, q)
            if c in ARRIVE[1:]:
                keep(c, apply_outer(c), True)
            else:
                keep(c, apply_neighbours(now, c), True)
            if c % 2 == 1:
                finish(c // 2)
            if c in LEAVE:
                q = LEAVE.index(c)
                send(later, q)
                wait_chunk(now, q, send_sems)
        return carry

    lax.fori_loop(0, SWEEPS - 1, step, 0)

    end = (SWEEPS - 1) % 2
    for p in range(pairs):
        for half in range(2):
            for l in range(loads):
                row = 8 * half + l
                coarse_ref[2 * p + half, l] = solution_v[p, row : row + 1, 0:values]
    for q in range(3):
        wait_chunk(end, q, recv_sems)
        wait_chunk(end, q, send_sems)
    around = jnp.concatenate(
        [
            jnp.concatenate([column(end, d, p, 0), column(end, d, p, 1)], axis=1)
            for d in range(9)
            for p in range(pairs)
        ],
        axis=0,
    )
    fetched = dot(gather_v[...], around)[:, 0:values].astype(BF16)
    octant_up = jnp.concatenate([upright(octant)] * loads, axis=0)
    total = jnp.zeros((values, loads * slots), F32)
    for o in range(8):
        chosen = fetched * jnp.where(octant_up == o, 1.0, 0.0).astype(BF16)
        total += dot_nt(restrict_t[o], chosen)
    for l in range(loads):
        correction_ref[l] = total[:, l * slots : (l + 1) * slots] * mask


def local(fine_list, fine_residual, solid_bits, restrict_ops, operator, pattern):
    slots, loads, values = fine_residual.shape
    bricks = operator.shape[2]
    pairs = bricks // 2
    rows = bricks * 8
    any_space = pl.BlockSpec(memory_space=pl.ANY)
    vmem = pl.BlockSpec(memory_space=pltpu.VMEM)
    dma = pltpu.SemaphoreType.DMA
    correction, coarse = pl.pallas_call(
        kernel,
        out_shape=[
            jax.ShapeDtypeStruct((loads, values, slots), F32),
            jax.ShapeDtypeStruct((bricks, loads, 1, values), F32),
        ],
        in_specs=[any_space] * 6,
        out_specs=[vmem, vmem],
        scratch_shapes=[
            pltpu.VMEM((1, slots), jnp.int32),
            pltpu.VMEM((3, slots), jnp.int32),
            pltpu.VMEM((loads, values, slots), F32),
            pltpu.VMEM((8, values, values), F32),
            pltpu.VMEM((bricks, values, values), BF16),
            pltpu.VMEM((bricks, 1, 26), jnp.int32),
            pltpu.VMEM((16, 128), jnp.int32),
            pltpu.SMEM((16, 128), jnp.int32),
            pltpu.VMEM((bricks, values, 41 * 128), BF16),
            pltpu.VMEM((8, values, values), BF16),
            pltpu.VMEM((8, values, values), BF16),
            pltpu.VMEM((loads * slots, 9 * rows), BF16),
            pltpu.VMEM((3, 48, 128), F32),
            pltpu.VMEM((8, 3, 48, 128), BF16),
            pltpu.VMEM((8, 3, 48, 128), BF16),
            pltpu.VMEM((2, 8, pairs, 2, 16, 128), BF16),
            pltpu.VMEM((2, pairs, 2, 16, 128), BF16),
            pltpu.VMEM((9, pairs, 16, 128), BF16),
            pltpu.VMEM((5, pairs, 16, 128), BF16),
            pltpu.VMEM((pairs, 16, 256), F32),
            pltpu.VMEM((pairs, 16, 256), F32),
            pltpu.VMEM((pairs, 16, 256), F32),
            pltpu.VMEM((pairs, 16, 256), F32),
            dma((6,)),
            dma((bricks,)),
            dma,
            dma((2, 3)),
            dma((2, 3)),
            dma((2, 3)),
        ]
        + [pltpu.VMEM((26, values, values), BF16)] * bricks,
        compiler_params=pltpu.CompilerParams(
            collective_id=0, has_side_effects=True, vmem_limit_bytes=63 * 2**20
        ),
    )(
        fine_list.reshape(1, slots),
        solid_bits.T,
        fine_residual.transpose(1, 2, 0),
        restrict_ops,
        operator.reshape(bricks, 27, values, values),
        pattern.reshape(bricks, 1, 26),
    )
    return correction.transpose(2, 0, 1), coarse.reshape(1, 1, bricks, loads, values)


def solution(mesh):
    in_specs = (
        P(("gx", "gy")),
        P(("gx", "gy"), None, None),
        P(("gx", "gy"), None),
        P(),
        P("gx", "gy", None, None, None, None),
        P("gx", "gy", None, None),
    )
    out_specs = (P(("gx", "gy"), None, None), P("gx", "gy", None, None, None))
    return jax.shard_map(local, mesh=mesh, in_specs=in_specs, out_specs=out_specs, check_vma=False)
```

```python
import functools
import jax
import jax.numpy as jnp
from jax import lax
from jax.experimental import pallas as pl
from jax.experimental.pallas import tpu as pltpu
from jax.sharding import PartitionSpec as P

SWEEPS = 8
DAMPING = 0.8
OFFSETS = [(dx, dy) for dx in (-1, 0, 1) for dy in (-1, 0, 1)]
OWN = 4
NEIGHBOURS = [d for d in range(9) if d != OWN]
ARRIVE = (0, 3, 7)
LEAVE = (4, 7, 11)
AHEAD = 6
SLOT = {d: (d if d < OWN else d - 1) for d in range(9) if d != OWN}
JOINED = ((0, 1), (2, 3), (5, 6), (7, 8))
NT = (((1,), (1,)), ((), ()))
F32 = jnp.float32
BF16 = jnp.bfloat16


def dot(a, b):
    return jnp.dot(a, b, preferred_element_type=F32)


def dot_nt(a, b):
    return lax.dot_general(a, b, NT, preferred_element_type=F32)


def swapped(tile):
    return jnp.concatenate([tile[8:16], tile[0:8]], axis=0)


def kernel(
    list_hbm, bits_hbm, residual_hbm, restrict_hbm, operator_hbm, pattern_hbm,
    correction_ref, coarse_ref,
    list_v, bits_v, residual_v, restrict_v, own_v, pattern_v, inverse_v, inverse_s,
    packed, restrict_b, restrict_t, gather_v, rhs_own, rhs_send, rhs_land,
    land, own, turned, joined, applied_v, solution_v, rhs_v, scale_v,
    small_sem, raw_sem, inverse_sem, rhs_sems, send_sems, recv_sems,
    *raw,
):
    bricks = len(raw)
    pairs = bricks // 2
    loads = residual_v.shape[0]
    values = restrict_v.shape[1]
    slots = list_v.shape[1]
    rows = bricks * 8
    count_x = lax.axis_size("gx")
    count_y = lax.axis_size("gy")
    here_x = lax.axis_index("gx")
    here_y = lax.axis_index("gy")

    small = [
        pltpu.make_async_copy(src, dst, small_sem.at[i])
        for i, (src, dst) in enumerate(
            [
                (pattern_hbm, pattern_v),
                (list_hbm, list_v),
                (bits_hbm, bits_v),
                (residual_hbm, residual_v),
                (restrict_hbm, restrict_v),
                (operator_hbm.at[:, 0], own_v),
            ]
        )
    ]
    for copy in small:
        copy.start()
    big = [
        pltpu.make_async_copy(operator_hbm.at[c, pl.ds(1, 26)], raw[c], raw_sem.at[c])
        for c in range(bricks)
    ]

    land[...] = jnp.zeros(land.shape, BF16)
    rhs_land[...] = jnp.zeros(rhs_land.shape, BF16)

    applied_v[...] = jnp.zeros(applied_v.shape, F32)

    inside = {}
    around_x = 3 - (here_x == 0).astype(jnp.int32) - (here_x == count_x - 1).astype(jnp.int32)
    around_y = 3 - (here_y == 0).astype(jnp.int32) - (here_y == count_y - 1).astype(jnp.int32)
    beside = around_x * around_y - 1
    for d, (dx, dy) in enumerate(OFFSETS):
        to_x = here_x + dx
        to_y = here_y + dy
        if d != OWN:
            inside[d] = (to_x >= 0) & (to_x < count_x) & (to_y >= 0) & (to_y < count_y)

    def to_each(action):
        for d in (0, 2, 6, 8, 3, 5, 1, 7):
            dx, dy = OFFSETS[d]

            @pl.when(inside[d])
            def _():
                action(d, (here_x + dx, here_y + dy))

    def wait_each(part, sem):
        for count in (8, 5, 3):

            @pl.when(beside == count)
            def _():
                some = part.at[pl.ds(0, count)]
                pltpu.make_async_copy(some, some, sem).wait()

    barrier = pltpu.get_barrier_semaphore()
    to_each(
        lambda d, target: pl.semaphore_signal(
            barrier, inc=1, device_id=target, device_id_type=pl.DeviceIdType.MESH
        )
    )

    small[0].wait()
    pattern = pattern_v[...].reshape(bricks, 26)
    lane = lax.broadcasted_iota(jnp.int32, (bricks, 26), 1)
    wide = lax.broadcasted_iota(jnp.int32, (bricks, 128), 1)
    inverse = jnp.zeros((bricks, 128), jnp.int32)
    for t in range(26):
        at = jnp.max(jnp.where(pattern == t, lane, 0), axis=1, keepdims=True)
        inverse = jnp.where(wide == t, at, inverse)
    inverse_v[...] = jnp.zeros(inverse_v.shape, jnp.int32)
    inverse_v[0:bricks] = inverse
    inverse_copy = pltpu.make_async_copy(inverse_v, inverse_s, inverse_sem)
    inverse_copy.start()

    small[1].wait()
    small[2].wait()
    entry = list_v[...]
    live = entry >= 0
    brick = entry >> 3
    octant = jnp.where(live, entry & 7, -1)
    line = (brick * 43691) >> 19
    pos_z = brick - line * bricks
    step_x = (line >> 4) - here_x
    step_y = (line & 15) - here_y
    dest = ((step_x + 1) * 3 + step_y + 1) * bricks + pos_z
    dest = jnp.where(live, dest, -8)

    node = lax.broadcasted_iota(jnp.int32, (values // 3, slots), 0)
    word = jnp.where(
        node < 30, bits_v[0:1, :], jnp.where(node < 60, bits_v[1:2, :], bits_v[2:3, :])
    )
    shift = node - jnp.where(node >= 30, 30, 0) - jnp.where(node >= 60, 30, 0)
    flags = (lax.shift_right_logical(word, shift) & 1).astype(F32)
    flags = jnp.where(live, flags, 0.0)
    mask = jnp.concatenate([flags, flags, flags], axis=0)

    small[3].wait()
    masked = jnp.concatenate(
        [(residual_v[l] * mask).astype(BF16) for l in range(loads)], axis=1
    )
    small[4].wait()
    for c in range(AHEAD):
        big[c].start()
    octants = jnp.concatenate([octant] * loads, axis=1)
    restricted = jnp.zeros((values, loads * slots), F32)
    for o in range(8):
        matrix = restrict_v[o].astype(BF16)
        restrict_b[o] = matrix
        chosen = masked * jnp.where(octants == o, 1.0, 0.0).astype(BF16)
        restricted += dot(matrix, chosen)
    key = jnp.concatenate([dest * 8 + l for l in range(loads)], axis=1)
    row_id = lax.broadcasted_iota(jnp.int32, (9 * rows, loads * slots), 0)
    summing = jnp.where(row_id == key, 1.0, 0.0).astype(BF16)
    outgoing = dot_nt(summing, restricted.astype(BF16))
    low = lax.broadcasted_iota(jnp.int32, (16, 128), 1) < 64
    for d in range(9):
        for q in range(3):
            at = d * rows + 32 * q
            part = outgoing[at : at + 32]
            tail = jnp.concatenate([part[:, 128:values], jnp.zeros((32, 256 - values), F32)], axis=1)
            tail = jnp.where(low, tail[0:16], pltpu.roll(tail[16:32], 64, 1))
            if d == OWN:
                rhs_own[q, 0:32] = part[:, 0:128]
                rhs_own[q, 32:48] = tail
            else:
                rhs_send[SLOT[d], q, 0:32] = part[:, 0:128].astype(BF16)
                rhs_send[SLOT[d], q, 32:48] = tail.astype(BF16)

    inverse_copy.wait()
    small[5].wait()

    def block_of(c, d, dz):
        t = d * 3 + dz + 1
        if t == 13:
            return own_v.at[c]
        return raw[c].at[inverse_s[c, t - (1 if t > 13 else 0)]]

    def repack(c):
        big[c].wait()
        if c + AHEAD < bricks:
            big[c + AHEAD].start()
        partner = 1 if c % 2 == 0 else -1
        edge = c == 0 or c == bricks - 1

        def put(at, value):
            packed[c, :, at * 128 : (at + 1) * 128] = value

        def halves(left, right):
            return jnp.concatenate([left[:, 128:values], right[:, 128:values]], axis=1)

        at = 0
        here = block_of(c, OWN, 0)
        near = block_of(c, OWN, partner)
        put(0, here[:, 0:128])
        put(1, halves(here, near))
        put(2, near[:, 0:128])
        at = 3
        if not edge:
            far = block_of(c, OWN, -partner)
            put(3, far[:, 0:128])
            last = far[:, 128:values]
            put(4, jnp.concatenate([last, jnp.zeros_like(last)], axis=1))
            at = 5
        for i, d in enumerate(NEIGHBOURS):
            here = block_of(c, d, 0)
            near = block_of(c, d, partner)
            put(at + i, here[:, 0:128])
            put(at + 8 + i, halves(here, near))
            put(at + 16 + i, near[:, 0:128])
            if not edge:
                put(at + 24 + i, block_of(c, d, -partner)[:, 0:128])
        if not edge:
            for i, (d, e) in enumerate(JOINED):
                put(at + 32 + i, halves(block_of(c, d, -partner), block_of(c, e, -partner)))

    for c in range(3):
        repack(c)

    pl.semaphore_wait(barrier, beside)
    for q in range(3):
        to_each(
            lambda d, target, q=q: pltpu.make_async_remote_copy(
                src_ref=rhs_send.at[SLOT[d], q],
                dst_ref=rhs_land.at[SLOT[8 - d], q],
                send_sem=rhs_sems.at[0, q],
                recv_sem=rhs_sems.at[1, q],
                device_id=target,
                device_id_type=pl.DeviceIdType.MESH,
            ).start()
        )

    for c in range(3, 7):
        repack(c)

    square = lax.broadcasted_iota(jnp.int32, (slots, slots), 0) == lax.broadcasted_iota(
        jnp.int32, (slots, slots), 1
    )

    def upright(row):
        return jnp.sum(
            jnp.where(square, row.astype(F32), 0.0), axis=1, keepdims=True
        ).astype(jnp.int32)

    dest_up = upright(dest)
    column_id = lax.broadcasted_iota(jnp.int32, (slots, 9 * rows), 1)
    for l in range(loads):
        gather_v[l * slots : (l + 1) * slots, :] = jnp.where(
            column_id == dest_up * 8 + l, 1.0, 0.0
        ).astype(BF16)
    diagonal = lax.broadcasted_iota(jnp.int32, (values, values), 0) == lax.broadcasted_iota(
        jnp.int32, (values, values), 1
    )
    unit = jnp.where(diagonal, 1.0, 0.0).astype(BF16)
    for o in range(8):
        restrict_t[o] = dot_nt(unit, restrict_b[o]).astype(BF16)

    for p in range(pairs):
        halves = []
        for c in (2 * p, 2 * p + 1):
            found = jnp.sum(
                jnp.where(diagonal, own_v[c].astype(F32), 0.0), axis=0, keepdims=True
            )
            halves.append(jnp.broadcast_to(DAMPING / found, (8, values)))
        scale = jnp.concatenate(halves, axis=0)
        scale_v[p, :, 0:128] = scale[:, 0:128]
        scale_v[p, :, 128:256] = jnp.concatenate(
            [scale[:, 128:values], jnp.zeros((16, 256 - values), F32)], axis=1
        )

    def publish(par, p, value):
        tail = value[:, 128:256]
        own[par, p, 0] = value[:, 0:128].astype(BF16)
        own[par, p, 1] = jnp.where(low, tail, pltpu.roll(swapped(tail), 64, 1)).astype(BF16)
        turned[OWN, p] = swapped(value[:, 0:128]).astype(BF16)
        joined[len(JOINED), p] = swapped(tail).astype(BF16)

    def send(par, q):
        to_each(
            lambda d, target: pltpu.make_async_remote_copy(
                src_ref=own.at[par, pl.ds(2 * q, 2)],
                dst_ref=land.at[par, SLOT[8 - d], pl.ds(2 * q, 2)],
                send_sem=send_sems.at[par, q],
                recv_sem=recv_sems.at[par, q],
                device_id=target,
                device_id_type=pl.DeviceIdType.MESH,
            ).start()
        )

    def wait_chunk(par, q, sems):
        wait_each(land.at[par, :, pl.ds(2 * q, 2)], sems.at[par, q])

    def column(par, d, p, kind):
        return own[par, p, kind] if d == OWN else land[par, SLOT[d], p, kind]

    for q in range(3):
        wait_each(rhs_land.at[:, q], rhs_sems.at[1, q])
        total = rhs_own[q]
        for s in range(8):
            total += rhs_land[s, q].astype(F32)
        tails = (total[32:48], pltpu.roll(total[32:48], 64, 1))
        for half in range(2):
            p = 2 * q + half
            rhs = jnp.concatenate([total[16 * half : 16 * half + 16], tails[half]], axis=1)
            rhs_v[p] = rhs
            first = scale_v[p] * rhs
            solution_v[p] = first
            publish(0, p, first)
        send(0, q)
    for q in range(3):
        wait_each(rhs_send.at[:, q], rhs_sems.at[0, q])

    for c in range(7, bricks):
        repack(c)

    def expand(par, q):
        for p in (2 * q, 2 * q + 1):
            for d in NEIGHBOURS:
                turned[d, p] = swapped(land[par, SLOT[d], p, 0].astype(F32)).astype(BF16)
            for i, (d, e) in enumerate(JOINED):
                left = land[par, SLOT[d], p, 1].astype(F32)
                right = land[par, SLOT[e], p, 1].astype(F32)
                joined[i, p] = jnp.where(low, pltpu.roll(left, 64, 1), right).astype(BF16)

    def inner_tiles(par, c, columns):
        p = c // 2
        tiles = [column(par, d, p, 0) for d in columns]
        tiles += [column(par, d, p, 1) for d in columns]
        return tiles + [turned[d, p] for d in columns]

    def outer_tiles(c, columns, pairs_joined):
        if c == 0 or c == bricks - 1:
            return []
        other = c // 2 - 1 if c % 2 == 0 else c // 2 + 1
        return [turned[d, other] for d in columns] + [joined[i, other] for i in pairs_joined]

    def multiply(c, at, tiles):
        depth = 128 * len(tiles)
        return dot_nt(jnp.concatenate(tiles, axis=1), packed[c, :, 128 * at : 128 * at + depth])

    def apply_own(par, c):
        return multiply(c, 0, inner_tiles(par, c, [OWN]) + outer_tiles(c, [OWN], [len(JOINED)]))

    def neighbours_at(c):
        return 3 if c == 0 or c == bricks - 1 else 5

    def apply_inner(par, c):
        return multiply(c, neighbours_at(c), inner_tiles(par, c, NEIGHBOURS))

    def apply_outer(c):
        return multiply(c, neighbours_at(c) + 24, outer_tiles(c, NEIGHBOURS, range(len(JOINED))))

    def apply_neighbours(par, c):
        tiles = inner_tiles(par, c, NEIGHBOURS) + outer_tiles(c, NEIGHBOURS, range(len(JOINED)))
        return multiply(c, neighbours_at(c), tiles)

    def step(e, carry):
        now = lax.rem(e, 2)
        later = 1 - now

        def keep(c, result, add):
            part = slice(0, 8) if c % 2 == 0 else slice(8, 16)
            for lanes in (slice(0, 128), slice(128, values)):
                kept = result[part, lanes]
                if add:
                    kept += applied_v[c // 2, part, lanes]
                applied_v[c // 2, part, lanes] = kept

        def finish(p):
            value = solution_v[p] + scale_v[p] * (rhs_v[p] - applied_v[p])
            solution_v[p] = value
            publish(later, p, value)

        for c in range(bricks):
            keep(c, apply_own(now, c), False)
        for c in range(bricks):
            if c in ARRIVE:
                q = ARRIVE.index(c)
                if q > 0:
                    keep(c, apply_inner(now, c), True)
                wait_chunk(now, q, recv_sems)
                expand(now, q)
            if c in ARRIVE[1:]:
                keep(c, apply_outer(c), True)
            else:
                keep(c, apply_neighbours(now, c), True)
            if c % 2 == 1:
                finish(c // 2)
            if c in LEAVE:
                q = LEAVE.index(c)
                send(later, q)
                wait_chunk(now, q, send_sems)
        return carry

    lax.fori_loop(0, SWEEPS - 1, step, 0)

    end = (SWEEPS - 1) % 2
    for p in range(pairs):
        for half in range(2):
            for l in range(loads):
                row = 8 * half + l
                coarse_ref[2 * p + half, l] = solution_v[p, row : row + 1, 0:values]
    octant_up = jnp.concatenate([upright(octant)] * loads, axis=0)
    for q in range(3):
        wait_chunk(end, q, recv_sems)
        wait_chunk(end, q, send_sems)
    around = jnp.concatenate(
        [
            jnp.concatenate([column(end, d, p, 0), column(end, d, p, 1)], axis=1)
            for d in range(9)
            for p in range(pairs)
        ],
        axis=0,
    )
    fetched = dot(gather_v[...], around)[:, 0:values].astype(BF16)
    total = jnp.zeros((values, loads * slots), F32)
    for o in range(8):
        chosen = fetched * jnp.where(octant_up == o, 1.0, 0.0).astype(BF16)
        total += dot_nt(restrict_t[o], chosen)
    for l in range(loads):
        correction_ref[l] = total[:, l * slots : (l + 1) * slots] * mask


def local(fine_list, fine_residual, solid_bits, restrict_ops, operator, pattern):
    slots, loads, values = fine_residual.shape
    bricks = operator.shape[2]
    pairs = bricks // 2
    rows = bricks * 8
    any_space = pl.BlockSpec(memory_space=pl.ANY)
    vmem = pl.BlockSpec(memory_space=pltpu.VMEM)
    dma = pltpu.SemaphoreType.DMA
    correction, coarse = pl.pallas_call(
        kernel,
        out_shape=[
            jax.ShapeDtypeStruct((loads, values, slots), F32),
            jax.ShapeDtypeStruct((bricks, loads, 1, values), F32),
        ],
        in_specs=[any_space] * 6,
        out_specs=[vmem, vmem],
        scratch_shapes=[
            pltpu.VMEM((1, slots), jnp.int32),
            pltpu.VMEM((3, slots), jnp.int32),
            pltpu.VMEM((loads, values, slots), F32),
            pltpu.VMEM((8, values, values), F32),
            pltpu.VMEM((bricks, values, values), BF16),
            pltpu.VMEM((bricks, 1, 26), jnp.int32),
            pltpu.VMEM((16, 128), jnp.int32),
            pltpu.SMEM((16, 128), jnp.int32),
            pltpu.VMEM((bricks, values, 41 * 128), BF16),
            pltpu.VMEM((8, values, values), BF16),
            pltpu.VMEM((8, values, values), BF16),
            pltpu.VMEM((loads * slots, 9 * rows), BF16),
            pltpu.VMEM((3, 48, 128), F32),
            pltpu.VMEM((8, 3, 48, 128), BF16),
            pltpu.VMEM((8, 3, 48, 128), BF16),
            pltpu.VMEM((2, 8, pairs, 2, 16, 128), BF16),
            pltpu.VMEM((2, pairs, 2, 16, 128), BF16),
            pltpu.VMEM((9, pairs, 16, 128), BF16),
            pltpu.VMEM((5, pairs, 16, 128), BF16),
            pltpu.VMEM((pairs, 16, 256), F32),
            pltpu.VMEM((pairs, 16, 256), F32),
            pltpu.VMEM((pairs, 16, 256), F32),
            pltpu.VMEM((pairs, 16, 256), F32),
            dma((6,)),
            dma((bricks,)),
            dma,
            dma((2, 3)),
            dma((2, 3)),
            dma((2, 3)),
        ]
        + [pltpu.VMEM((26, values, values), BF16)] * bricks,
        compiler_params=pltpu.CompilerParams(
            collective_id=0, has_side_effects=True, vmem_limit_bytes=63 * 2**20
        ),
    )(
        fine_list.reshape(1, slots),
        solid_bits.T,
        fine_residual.transpose(1, 2, 0),
        restrict_ops,
        operator.reshape(bricks, 27, values, values),
        pattern.reshape(bricks, 1, 26),
    )
    return correction.transpose(2, 0, 1), coarse.reshape(1, 1, bricks, loads, values)


def solution(mesh):
    in_specs = (
        P(("gx", "gy")),
        P(("gx", "gy"), None, None),
        P(("gx", "gy"), None),
        P(),
        P("gx", "gy", None, None, None, None),
        P("gx", "gy", None, None),
    )
    out_specs = (P(("gx", "gy"), None, None), P("gx", "gy", None, None, None))
    return jax.shard_map(local, mesh=mesh, in_specs=in_specs, out_specs=out_specs, check_vma=False)
```
